32 devices in a mesh: groups: 2 (over x), rows: 8 (over z, y), cols: 2 (over core).
Axes of the slice: x: 2, y: 2, z: 4, core: 2. Of those that a mesh axis runs over, the one named last changes fastest.
Arguments:
- depth: float32 [4096, 512], P(('groups', 'rows'), 'cols'), parts along dimension 0, may hold values from 0 to 1.5, as said below
- velocity: float32 [2, 4096, 512], P(None, ('groups', 'rows'), 'cols'), parts along dimension 1, may hold values from -1 to 1
- bed: float32 [4096, 512], P(('groups', 'rows'), 'cols'), parts along dimension 0, may hold values from 0 to 0.5
- slots: int32 [16, 2, 3], P(('groups', 'rows'), 'cols'), parts along dimension 0, may hold values from -1 to 63, as said below
Outputs:
- packed: float32 [16, 2, 3, 3, 128, 128], P(('groups', 'rows'), 'cols'), parts along dimension 0
The draws below stay inside these ranges and needn't reach their ends.
There are 2 independent parts, one for each index of `groups`. The reference program is written for one: setup_inputs(seed, part) draws one part's arguments, and reference() takes and returns one part's arrays. A program takes and returns all parts, laid end to end along the dimension named above; each array names one. Nothing has to cross between parts.
Inputs may be any that keep to these rules, and one draw needn't show every extreme that they name: Each non-negative entry of slots[r, c] is the id of a tile of device (r, c)'s own block (tile rows r * 2 to r * 2 + 1, tile columns c * 2 to c * 2 + 1) or of the block of its partner, device ((r + 4) mod 8, c). No id is listed twice. Every device's partner lists at least one and at most 2 tiles of that device's block, and some device's partner lists exactly 2; at most 3 entries of one list are ids, and some list has exactly 3. `depth`: depth is zero on every cell of a tile that no slot list names.
All inputs are finite; a program needn't handle non-finite values.
Results may differ from the reference program's by a relative error of at most 0.0003.
Values sent between devices are 32-bit elements; how exact they have to be, the bound alone decides.
A program may use at most 64 MiB of HBM per device.

```python
import jax
import jax.numpy as jnp

TILE = 128
RT = 2
CT = 2
SLOTS = 3
GRID_ROWS = 2048
GRID_COLS = 512
N_ROWS = 8
N_COLS = 2


def tile_layout(key):
    half = N_ROWS // 2
    per_device = RT * CT
    pair_count = half * N_COLS
    keys = jax.random.split(key, 6)
    heavy_wet = jax.random.randint(keys[0], (pair_count,), per_device // 2, per_device + 1)
    light_wet = jax.random.randint(keys[1], (pair_count,), 1, per_device // 2 + 1)
    first_pair = jax.random.randint(keys[2], (), 0, pair_count)
    second_pair = (first_pair + 1 + jax.random.randint(keys[3], (), 0, pair_count - 1)) % pair_count
    pair_ids = jnp.arange(pair_count)
    heavy_wet = jnp.where(pair_ids == first_pair, per_device, heavy_wet)
    light_wet = jnp.where(pair_ids == first_pair, 1, light_wet)
    heavy_wet = jnp.where(pair_ids == second_pair, per_device, heavy_wet)
    light_wet = jnp.where(pair_ids == second_pair, per_device // 2, light_wet)
    top_heavy = jax.random.randint(keys[4], (pair_count,), 0, 2)
    heavy_send = (heavy_wet - light_wet) // 2 + 1
    light_send = jnp.ones_like(heavy_send)
    top_wet = jnp.where(top_heavy == 1, heavy_wet, light_wet)
    bottom_wet = jnp.where(top_heavy == 1, light_wet, heavy_wet)
    top_send = jnp.where(top_heavy == 1, heavy_send, light_send)
    bottom_send = jnp.where(top_heavy == 1, light_send, heavy_send)
    wet_count = jnp.concatenate([top_wet.reshape(half, N_COLS), bottom_wet.reshape(half, N_COLS)], axis=0)
    sent_count = jnp.concatenate([top_send.reshape(half, N_COLS), bottom_send.reshape(half, N_COLS)], axis=0)
    scores = jax.random.randint(keys[5], (N_ROWS, N_COLS, per_device), 0, 2 ** 20) * per_device + jnp.arange(per_device)
    order = jnp.argsort(scores, axis=-1)
    ranks = jnp.argsort(order, axis=-1)
    wet = ranks < wet_count[..., None]
    position = jnp.cumsum(wet.astype(jnp.int32), axis=-1) - 1
    sent = wet & (position >= (wet_count - sent_count)[..., None])
    return (wet, sent)


def draw_slots(key, part):
    wet, sent = tile_layout(jax.random.fold_in(key, 7))
    per_device = RT * CT
    half = N_ROWS // 2
    tile_cols_all = CT * N_COLS
    row_ids = jnp.arange(N_ROWS)[:, None, None]
    col_ids = jnp.arange(N_COLS)[None, :, None]
    local = jnp.arange(per_device)[None, None, :]
    global_ids = (row_ids * RT + local // CT) * tile_cols_all + col_ids * CT + local % CT
    kept = wet & jnp.logical_not(sent)
    taken = jnp.roll(sent, half, axis=0)
    taken_ids = jnp.roll(global_ids, half, axis=0)
    candidate_ids = jnp.concatenate([global_ids, taken_ids], axis=-1)
    candidate_flags = jnp.concatenate([kept, taken], axis=-1).astype(jnp.int32)
    target = jnp.cumsum(candidate_flags, axis=-1) - 1
    target = jnp.where(candidate_flags == 1, target, SLOTS)
    hits = (target[..., :, None] == jnp.arange(SLOTS)[None, None, None, :]).astype(jnp.int32)
    return (jnp.sum(hits * (candidate_ids + 1)[..., None], axis=-2) - 1).astype(jnp.int32)


def draw_depth(key, part):
    wet, sent = tile_layout(jax.random.fold_in(key, 7))
    tiles = wet.reshape(N_ROWS, N_COLS, RT, CT).transpose(0, 2, 1, 3).reshape(N_ROWS * RT, N_COLS * CT).astype(jnp.float32)
    base_key, cell_key = jax.random.split(jax.random.fold_in(key, 11))
    cell_shape = (N_ROWS * RT * TILE, N_COLS * CT * TILE)
    base = jax.random.uniform(base_key, tiles.shape, jnp.float32, 0.2, 1.0)
    rough = jax.random.uniform(cell_key, cell_shape, jnp.float32, -0.4, 0.5)
    base_cells = jnp.repeat(jnp.repeat(base, TILE, axis=0), TILE, axis=1)
    wet_cells = jnp.repeat(jnp.repeat(tiles, TILE, axis=0), TILE, axis=1)
    return (wet_cells * jnp.maximum(0.0, base_cells + rough)).astype(jnp.float32)


def level_of(rng, dims, shards, smallest, high):
    gain, own = 1.0, jax.random.fold_in(rng, 6)
    for dim, parts in shards:
        heights = jnp.exp(jax.random.uniform(jax.random.fold_in(own, dim), (parts,), jnp.float32, smallest / len(shards), high / len(shards)))
        gain = gain * jnp.repeat(heights, dims[dim] // parts).reshape([-1 if axis == dim else 1 for axis in range(len(dims))])
    return gain


def setup_inputs(seed: int = 0, part: int = 0) -> dict:
    seeds = jax.random.split(jax.random.key(seed), 5)
    part_keys = jax.random.split(jax.random.fold_in(seeds[4], part), 5)
    return {
        "depth": draw_depth(jax.random.fold_in(jax.random.fold_in(seeds[4], part), 71), part),
        "velocity": jnp.clip(jax.random.uniform(part_keys[1], (2, GRID_ROWS, GRID_COLS), jnp.float32, -1.0, 1.0) * level_of(part_keys[1], (2, GRID_ROWS, GRID_COLS), ((1, 8), (2, 2)), -0.4, 0.0), -1.0, 1.0),
        "bed": jnp.clip(0.5 * jax.random.uniform(part_keys[2], (GRID_ROWS, GRID_COLS), jnp.float32) ** level_of(part_keys[2], (GRID_ROWS, GRID_COLS), ((0, 8), (1, 2)), -0.2, 0.2), 0.0, 0.5),
        "slots": draw_slots(jax.random.fold_in(jax.random.fold_in(seeds[4], part), 71), part),
    }


GRAVITY = 9.81
TIME_STEP = 0.04
DRY_DEPTH = 0.05
SPEED_FLOOR = 0.5

def take_range(values, lower_end, upper_end, direction):
    selector = [slice(None)] * values.ndim
    selector[direction] = slice(lower_end, upper_end)
    return values[tuple(selector)]

def minmod(left_diff, right_diff):
    return 0.5 * (jnp.sign(left_diff) + jnp.sign(right_diff)) * jnp.minimum(jnp.abs(left_diff), jnp.abs(right_diff))

def face_values(values, direction):
    change = take_range(values, 1, None, direction) - take_range(values, 0, -1, direction)
    slope = minmod(take_range(change, 0, -1, direction), take_range(change, 1, None, direction))
    middle = take_range(values, 1, -1, direction)
    return (middle - 0.5 * slope, middle + 0.5 * slope)

def velocity_from(water, flow):
    return 2.0 * water * flow / (water * water + jnp.maximum(water * water, DRY_DEPTH * DRY_DEPTH))

def flux_sweep(water, normal, across, ground, direction):
    water_low, water_high = face_values(water, direction)
    normal_low, normal_high = face_values(normal, direction)
    across_low, across_high = face_values(across, direction)
    ground_low, ground_high = face_values(ground, direction)

    def left_side(values):
        return take_range(values, 0, -1, direction)

    def right_side(values):
        return take_range(values, 1, None, direction)
    water_left = left_side(water_high)
    water_right = right_side(water_low)
    speed_left = velocity_from(water_left, left_side(normal_high))
    speed_right = velocity_from(water_right, right_side(normal_low))
    drift_left = velocity_from(water_left, left_side(across_high))
    drift_right = velocity_from(water_right, right_side(across_low))
    ground_left = left_side(ground_high)
    ground_right = right_side(ground_low)
    ground_top = jnp.maximum(ground_left, ground_right)
    level_left = jnp.maximum(0.0, water_left + ground_left - ground_top)
    level_right = jnp.maximum(0.0, water_right + ground_right - ground_top)
    wave_left = jnp.sqrt(GRAVITY * level_left)
    wave_right = jnp.sqrt(GRAVITY * level_right)
    lower_speed = jnp.minimum(jnp.minimum(speed_left - wave_left, speed_right - wave_right), 0.0)
    upper_speed = jnp.maximum(jnp.maximum(speed_left + wave_left, speed_right + wave_right), 0.0)
    spread = jnp.maximum(upper_speed - lower_speed, SPEED_FLOOR)

    def riemann_flux(flux_left, flux_right, kept_left, kept_right):
        return (upper_speed * flux_left - lower_speed * flux_right + upper_speed * lower_speed * (kept_right - kept_left)) / spread
    mass_left = level_left * speed_left
    mass_right = level_right * speed_right
    mass_flux = riemann_flux(mass_left, mass_right, level_left, level_right)
    push_flux = riemann_flux(mass_left * speed_left + 0.5 * GRAVITY * level_left * level_left, mass_right * speed_right + 0.5 * GRAVITY * level_right * level_right, mass_left, mass_right)
    side_flux = riemann_flux(mass_left * drift_left, mass_right * drift_right, level_left * drift_left, level_right * drift_right)

    def lower_face(values):
        return take_range(values, 0, -1, direction)

    def upper_face(values):
        return take_range(values, 1, None, direction)
    cell_low = take_range(water_low, 1, -1, direction)
    cell_high = take_range(water_high, 1, -1, direction)
    ground_cell_low = take_range(ground_low, 1, -1, direction)
    ground_cell_high = take_range(ground_high, 1, -1, direction)
    below_level = lower_face(level_right)
    above_level = upper_face(level_left)
    mass_rate = lower_face(mass_flux) - upper_face(mass_flux)
    push_rate = lower_face(push_flux) - upper_face(push_flux) + 0.5 * GRAVITY * (cell_low * cell_low - below_level * below_level) - 0.5 * GRAVITY * (cell_high * cell_high - above_level * above_level) + 0.5 * GRAVITY * (cell_low + cell_high) * (ground_cell_low - ground_cell_high)
    side_rate = lower_face(side_flux) - upper_face(side_flux)
    return (mass_rate, push_rate, side_rate)

def advance(state, statics):
    water = state[..., 0, :, :]
    flow_x = state[..., 1, :, :]
    flow_y = state[..., 2, :, :]
    ground = statics[..., 0, :, :]
    active = statics[..., 1, :, :]

    def rows_inner(values):
        return values[..., 2:-2, :]

    def cols_inner(values):
        return values[..., :, 2:-2]

    def center(values):
        return values[..., 2:-2, 2:-2]
    mass_x, push_x, side_x = flux_sweep(rows_inner(water), rows_inner(flow_x), rows_inner(flow_y), rows_inner(ground), -1)
    mass_y, push_y, side_y = flux_sweep(cols_inner(water), cols_inner(flow_y), cols_inner(flow_x), cols_inner(ground), -2)
    new_water = center(water) + TIME_STEP * (mass_x + mass_y)
    new_flow_x = center(flow_x) + TIME_STEP * (push_x + side_y)
    new_flow_y = center(flow_y) + TIME_STEP * (side_x + push_y)
    updated = jnp.stack([new_water, new_flow_x, new_flow_y], axis=-3)
    keeping = center(active)[..., None, :, :] > 0.5
    return jnp.where(keeping, updated, center(state))

def reference(depth, velocity, bed, slots):
    state = jnp.stack([depth, depth * velocity[0], depth * velocity[1]])
    tile_rows = depth.shape[0] // TILE
    tile_cols = depth.shape[1] // TILE
    tile_total = tile_rows * tile_cols
    listed = slots.reshape(-1)
    targets = jnp.where(listed >= 0, listed, tile_total).astype(jnp.int32)
    flags = jnp.zeros((tile_total + 1,), jnp.float32).at[targets].set(1.0)[:tile_total]
    active_tiles = flags.reshape(tile_rows, tile_cols)
    active_cells = jnp.repeat(jnp.repeat(active_tiles, TILE, axis=0), TILE, axis=1)
    statics = jnp.pad(jnp.stack([bed, active_cells]), ((0, 0), (2, 2), (2, 2)))
    for sweep_index in range(2):
        state = advance(jnp.pad(state, ((0, 0), (2, 2), (2, 2))), statics)
    tiles = state.reshape(3, tile_rows, TILE, tile_cols, TILE).transpose(1, 3, 0, 2, 4).reshape(tile_total, 3, TILE, TILE)
    chosen = tiles[jnp.maximum(listed, 0).astype(jnp.int32)] * (listed >= 0).astype(jnp.float32)[:, None, None, None]
    return chosen.reshape(slots.shape + (3, TILE, TILE))
```

```python
import functools

import jax
import jax.numpy as jnp
from jax import lax
from jax.experimental import pallas as pl
from jax.experimental.pallas import tpu as pltpu
from jax.sharding import PartitionSpec as P

TILE = 128
RT = 2
CT = 2

GRAVITY = 9.81
TIME_STEP = 0.04
DRY_DEPTH = 0.05
SPEED_FLOOR = 0.5
BANDS = 18
ROWS = 8 * BANDS
MESH = pl.DeviceIdType.MESH


def minmod(a, b):
    return jnp.maximum(jnp.minimum(a, b), 0.0) + jnp.minimum(jnp.maximum(a, b), 0.0)


def face_sweep(own, below, slope, slope_below):
    half = [0.5 * s for s in slope]
    low = [v - s for v, s in zip(own, half)]
    high = [v + 0.5 * s for v, s in zip(below, slope_below)]

    def speeds(h, n, t):
        square = h * h
        w = 2.0 * h / (square + jnp.maximum(square, DRY_DEPTH * DRY_DEPTH))
        return w * n, w * t

    hl, nl, tl, zl = high
    hr, nr, tr, zr = low
    ul, vl = speeds(hl, nl, tl)
    ur, vr = speeds(hr, nr, tr)
    top = jnp.maximum(zl, zr)
    el = jnp.maximum(0.0, hl + zl - top)
    er = jnp.maximum(0.0, hr + zr - top)
    cl = jnp.sqrt(GRAVITY * el)
    cr = jnp.sqrt(GRAVITY * er)
    am = jnp.minimum(jnp.minimum(ul - cl, ur - cr), 0.0)
    ap = jnp.maximum(jnp.maximum(ul + cl, ur + cr), 0.0)
    inv = 1.0 / jnp.maximum(ap - am, SPEED_FLOOR)
    bp = ap * inv
    bm = am * inv
    bb = bp * am
    ml = el * ul
    mr = er * ur
    gl = 0.5 * GRAVITY * el * el
    gr = 0.5 * GRAVITY * er * er
    mass = bp * ml - bm * mr + bb * (er - el)
    push = bp * (ml * ul + gl) - bm * (mr * ur + gr) + bb * (mr - ml)
    side = bp * (ml * vl) - bm * (mr * vr) + bb * (er * vr - el * vl)
    cell_high = own[0] + half[0]
    total = hr + cell_high
    bedterm = 0.5 * GRAVITY * (total * (hr - cell_high) - 2.0 * total * half[3])
    return (mass, push + (bedterm - gr), side), (mass, push - gl, side)


def kernel(n, depth, vel, bed, lists, slots, out,
           strips, colpack, corner, rowgot, colgot, cornergot, listgot, ids,
           ext, tiles, work, mid, part, face, res,
           send_sem, recv_sem, id_sem):
    g = lax.axis_index("groups")
    r = lax.axis_index("rows")
    c = lax.axis_index("cols")
    peer = 1 - c
    half = n // 2
    shifts = (0, 1, n - 1, half, half + 1, half - 1)
    opposite = (0, 2, 1, 3, 5, 4)
    tile_cols_all = CT * 2

    def at(k, other):
        return (g, lax.rem(r + shifts[k], n), peer if other else c)

    barrier = pltpu.get_barrier_semaphore()
    for k in range(6):
        for o in range(2):
            if k or o:
                pl.semaphore_signal(barrier, inc=1, device_id=at(k, o), device_id_type=MESH)

    lane8 = lax.broadcasted_iota(jnp.int32, (8, 128), 1)
    fields = (lambda rs, ls: depth[rs, ls], lambda rs, ls: vel[0, rs, ls],
              lambda rs, ls: vel[1, rs, ls], lambda rs, ls: bed[rs, ls])
    left, right, both = pl.ds(0, 128), pl.ds(128, 128), pl.ds(0, 256)
    for f in range(4):
        for e, rs in enumerate((pl.ds(0, 8), pl.ds(248, 8))):
            strips[e, f] = fields[f](rs, both)
            corner[e, f] = jnp.where(c == 0, fields[f](rs, right), fields[f](rs, left))

    @pl.loop(0, 32)
    def _(b):
        rs = pl.ds(pl.multiple_of(8 * b, 8), 8)
        packed = jnp.zeros((8, 128), jnp.float32)
        for f in range(4):
            slab = jnp.where(c == 0, fields[f](rs, right), fields[f](rs, left))
            packed = jnp.where(lane8 // 8 == f, pltpu.roll(slab, 4 + 8 * f, 1), packed)
        colpack[rs, :] = packed

    pl.semaphore_wait(barrier, 11)

    copies = []

    def send(src, dst, k, o):
        i = len(copies)
        copy = pltpu.make_async_remote_copy(
            src_ref=src, dst_ref=dst, send_sem=send_sem.at[i], recv_sem=recv_sem.at[i],
            device_id=at(k, o), device_id_type=MESH)
        copy.start()
        copies.append(copy)

    send(colpack, colgot, 0, 1)
    send(strips.at[1], rowgot.at[0], 1, 0)
    send(strips.at[0], rowgot.at[1], 2, 0)
    send(corner.at[1], cornergot.at[0], 1, 1)
    send(corner.at[0], cornergot.at[1], 2, 1)
    for k in (3, 0, 1, 2, 4, 5):
        for o in range(2):
            if k or o:
                send(lists, listgot.at[2 * opposite[k] + o], k, o)
    listgot[0] = lists[...]

    @pl.loop(0, 32)
    def _(b):
        rs = pl.ds(pl.multiple_of(8 * b, 8), 8)
        rd = pl.ds(pl.multiple_of(8 * b + 8, 8), 8)
        for j, ls in enumerate((left, right)):
            d = depth[rs, ls]
            ext[0, j, rd, :] = d
            ext[1, j, rd, :] = d * vel[0, rs, ls]
            ext[2, j, rd, :] = d * vel[1, rs, ls]
            ext[3, j, rd, :] = bed[rs, ls]

    for f in range(5):
        work[f, 0:8] = jnp.zeros((8, 256), jnp.float32)
        work[f, ROWS + 8:ROWS + 16] = jnp.zeros((8, 256), jnp.float32)
        if f < 3:
            mid[f, 0:8] = jnp.zeros((8, 256), jnp.float32)
            mid[f, ROWS + 8:ROWS + 16] = jnp.zeros((8, 256), jnp.float32)
            face[f, ROWS + 8:ROWS + 16] = jnp.zeros((8, 256), jnp.float32)

    for copy in copies:
        copy.wait_recv()
    to_ids = pltpu.make_async_copy(listgot, ids, id_sem)
    to_ids.start()

    def put(j, rd, d, a, b, z, keep):
        d = jnp.where(keep, d, 0.0)
        ext[0, j, rd, :] = d
        ext[1, j, rd, :] = d * a
        ext[2, j, rd, :] = d * b
        ext[3, j, rd, :] = jnp.where(keep, z, 0.0)

    for e, (rd, keep) in enumerate(((pl.ds(0, 8), r > 0), (pl.ds(264, 8), r < n - 1))):
        for j, ls in enumerate((left, right)):
            put(j, rd, *(rowgot[e, f, :, ls] for f in range(4)), keep)
        put(2, rd, *(cornergot[e, f] for f in range(4)), keep)

    @pl.loop(0, 32)
    def _(b):
        rs = pl.ds(pl.multiple_of(8 * b, 8), 8)
        rd = pl.ds(pl.multiple_of(8 * b + 8, 8), 8)
        got = colgot[rs, :]
        put(2, rd, *(pltpu.roll(got, 128 - (4 + 8 * f), 1) for f in range(4)), True)

    to_ids.wait()

    def is_active(a, b):
        row = RT * r - 1 + a
        col = CT * c - 1 + b
        inside = (row >= 0) & (row < RT * n) & (col >= 0) & (col < tile_cols_all)
        ident = row * tile_cols_all + col
        k = {0: 2, 1: 0, 2: 0, 3: 1}[a]
        o = 0 if b in (1, 2) else 1
        partner = {0: 3, 1: 4, 2: 5}[k]
        hit = ids[2 * k + o, 0, 0] == ident
        for q in (k, partner):
            for s in range(3):
                hit = hit | (ids[2 * q + o, 0, s] == ident)
        return jnp.where(hit & inside, 1.0, 0.0)

    active = [[is_active(a, b) for b in range(4)] for a in range(4)]
    lower = lane8 < 64
    at_left = (c == 0)
    for i in range(2):
        for j in range(2):
            t = 2 * i + j

            def row_of(a):
                return jnp.broadcast_to(active[a][j + 1], (8, 128)), jnp.where(
                    lower, active[a][j + 2], active[a][j])

            top, middle, bottom = row_of(i), row_of(i + 1), row_of(i + 2)

            @pl.loop(0, BANDS)
            def _(b):
                rs = pl.ds(pl.multiple_of(8 * b, 8), 8)
                rd = pl.ds(pl.multiple_of(8 * b + 128 * i, 8), 8)
                for f in range(4):
                    tiles[t, f, rs, 0:128] = ext[f, j, rd, :]
                    outer = ext[f, 2, rd, :]
                    inner = ext[f, 1 - j, rd, :]
                    if j == 0:
                        tiles[t, f, rs, 128:256] = jnp.where(
                            lower, inner, jnp.where(at_left, 0.0, outer))
                    else:
                        tiles[t, f, rs, 128:256] = jnp.where(
                            lower, jnp.where(at_left, outer, 0.0), inner)
                for h in range(2):
                    tiles[t, 4, rs, 128 * h:128 * h + 128] = jnp.where(
                        b == 0, top[h], jnp.where(b == BANDS - 1, bottom[h], middle[h]))

    def owned(ident):
        safe = jnp.maximum(ident, 0)
        row = lax.div(safe, tile_cols_all)
        col = lax.rem(safe, tile_cols_all)
        mine = (ident >= 0) & (lax.div(row, RT) == r) & (lax.div(col, CT) == c)
        return mine, lax.rem(row, RT) * CT + lax.rem(col, CT)

    def ranked(entries):
        first = second = count = jnp.int32(0)
        for ident in entries:
            mine, tile = owned(ident)
            first = jnp.where(mine & (count == 0), tile, first)
            second = jnp.where(mine & (count == 1), tile, second)
            count = count + jnp.where(mine, 1, 0)
        return first, second

    sent = ranked([ids[6, 0, s] for s in range(3)])
    kept = ranked([slots[s] for s in range(3)])

    row8 = lax.broadcasted_iota(jnp.int32, (8, 256), 0)

    def from_next(cur, nxt):
        edge = row8[:, :cur.shape[1]] == 7
        return jnp.where(edge, pltpu.roll(nxt, 7, 0), pltpu.roll(cur, 7, 0))

    def step(src, bed_ref):
        refs = [src.at[0], src.at[1], src.at[2], bed_ref]
        order = (0, 2, 1, 3)

        def band(b, carry):
            prev_down, prev_slope = carry
            base = pl.multiple_of(8 * b + 8, 8)
            here = pl.ds(base, 8)
            ahead = pl.ds(pl.multiple_of(8 * b + 16, 8), 8)
            v0 = [ref[here, :] for ref in refs]
            down = [pltpu.roll(v, 1, 0) for v in v0]
            vm = [jnp.where(row8 == 0, p, d) for p, d in zip(prev_down, down)]
            vp = [from_next(v, ref[ahead, :]) for v, ref in zip(v0, refs)]
            slope = [minmod(v - m, p - v) for v, m, p in zip(v0, vm, vp)]
            turned = [pltpu.roll(q, 1, 0) for q in slope]
            slope_below = [jnp.where(row8 == 0, p, d) for p, d in zip(prev_slope, turned)]
            pick = lambda vs: [vs[q] for q in order]
            gain, loss = face_sweep(pick(v0), pick(vm), pick(slope), pick(slope_below))
            for q in range(3):
                face[q, here, :] = TIME_STEP * loss[order[q]]
            left_of = [pltpu.roll(v, 1, 1) for v in v0]
            diff = [x - y for x, y in zip(v0, left_of)]
            across = [minmod(d, pltpu.roll(d, 255, 1)) for d in diff]
            across_left = [pltpu.roll(q, 1, 1) for q in across]
            xgain, xloss = face_sweep(v0, left_of, across, across_left)
            for q in range(3):
                part[q, here, :] = v0[q] + TIME_STEP * (
                    xgain[q] + gain[order[q]] - pltpu.roll(xloss[q], 255, 1))
            return down, turned

        zeros = [jnp.zeros((8, 256), jnp.float32)] * 4
        lax.fori_loop(0, BANDS, band, (zeros, zeros))

    def task(k, carry):
        t = jnp.where(k == 0, sent[0], jnp.where(k == 1, sent[1], jnp.where(k == 2, kept[0], kept[1])))

        @pl.loop(0, BANDS)
        def _(b):
            rs = pl.ds(pl.multiple_of(8 * b, 8), 8)
            rd = pl.ds(pl.multiple_of(8 * b + 8, 8), 8)
            for f in range(5):
                work[f, rd, :] = tiles[t, f, rs, :]

        step(work, work.at[3])

        @pl.loop(0, BANDS)
        def _(b):
            rd = pl.ds(pl.multiple_of(8 * b + 8, 8), 8)
            ahead = pl.ds(pl.multiple_of(8 * b + 16, 8), 8)
            keep = work[4, rd, :] > 0.5
            for f in range(3):
                mid[f, rd, :] = jnp.where(
                    keep, part[f, rd, :] - from_next(face[f, rd, :], face[f, ahead, :]), work[f, rd, :])

        step(mid, work.at[3])

        @pl.loop(0, 16)
        def _(b):
            rd = pl.ds(pl.multiple_of(8 * b + 16, 8), 8)
            ahead = pl.ds(pl.multiple_of(8 * b + 24, 8), 8)
            for f in range(3):
                res[k, f, pl.ds(pl.multiple_of(8 * b, 8), 8), :] = (
                    part[f, rd, 0:128] - from_next(face[f, rd, 0:128], face[f, ahead, 0:128]))

        @pl.when(k < 2)
        def _():
            result_copy(k).start()

        return carry

    def result_copy(k):
        return pltpu.make_async_remote_copy(
            src_ref=res.at[k], dst_ref=res.at[4 + k], send_sem=send_sem.at[16 + k],
            recv_sem=recv_sem.at[16 + k], device_id=at(3, 0), device_id_type=MESH)

    lax.fori_loop(0, 4, task, 0)
    for k in range(2):
        result_copy(k).wait_recv()

    own_rank = far_rank = jnp.int32(0)
    for s in range(3):
        ident = slots[s]
        mine, _ = owned(ident)
        far = (ident >= 0) & jnp.logical_not(mine)
        index = jnp.where(mine, 2 + own_rank, jnp.where(far, 4 + far_rank, 2))
        index = jnp.minimum(index, 5)
        own_rank = own_rank + jnp.where(mine, 1, 0)
        far_rank = far_rank + jnp.where(far, 1, 0)

        @pl.loop(0, 16)
        def _(b):
            rs = pl.ds(pl.multiple_of(8 * b, 8), 8)
            for f in range(3):
                out[0, 0, s, f, rs, :] = jnp.where(ident >= 0, res[index, f, rs, :], 0.0)

    for copy in copies:
        copy.wait_send()
    for k in range(2):
        result_copy(k).wait_send()


def shards(depth, velocity, bed, slots):
    n = lax.axis_size("rows")
    listed = slots[0, 0]
    lists = jnp.pad(listed[None, :], ((0, 0), (0, 125)), constant_values=-1)
    vmem = pl.BlockSpec(memory_space=pltpu.VMEM)
    f32 = jnp.float32
    return pl.pallas_call(
        functools.partial(kernel, n),
        out_shape=jax.ShapeDtypeStruct((1, 1, 3, 3, TILE, TILE), f32),
        in_specs=[vmem] * 4 + [pl.BlockSpec(memory_space=pltpu.SMEM)],
        out_specs=vmem,
        scratch_shapes=[
            pltpu.VMEM((2, 4, 8, 256), f32),
            pltpu.VMEM((256, 128), f32),
            pltpu.VMEM((2, 4, 8, 128), f32),
            pltpu.VMEM((2, 4, 8, 256), f32),
            pltpu.VMEM((256, 128), f32),
            pltpu.VMEM((2, 4, 8, 128), f32),
            pltpu.VMEM((12, 1, 128), jnp.int32),
            pltpu.SMEM((12, 1, 128), jnp.int32),
            pltpu.VMEM((4, 3, 272, 128), f32),
            pltpu.VMEM((4, 5, ROWS, 256), f32),
            pltpu.VMEM((5, ROWS + 16, 256), f32),
            pltpu.VMEM((3, ROWS + 16, 256), f32),
            pltpu.VMEM((3, ROWS + 16, 256), f32),
            pltpu.VMEM((3, ROWS + 16, 256), f32),
            pltpu.VMEM((6, 3, TILE, TILE), f32),
            pltpu.SemaphoreType.DMA((18,)),
            pltpu.SemaphoreType.DMA((18,)),
            pltpu.SemaphoreType.DMA,
        ],
        compiler_params=pltpu.CompilerParams(
            collective_id=0, has_side_effects=True, vmem_limit_bytes=40 * 2**20),
    )(depth, velocity, bed, lists, listed)


def solution(mesh):
    in_specs = (
        P(("groups", "rows"), "cols"),
        P(None, ("groups", "rows"), "cols"),
        P(("groups", "rows"), "cols"),
        P(("groups", "rows"), "cols", None),
    )
    out_specs = P(("groups", "rows"), "cols", None, None, None, None)
    return jax.shard_map(shards, mesh=mesh, in_specs=in_specs, out_specs=out_specs, check_vma=False)
```

```python
import functools

import jax
import jax.numpy as jnp
from jax import lax
from jax.experimental import pallas as pl
from jax.experimental.pallas import tpu as pltpu
from jax.sharding import PartitionSpec as P

TILE = 128
RT = 2
CT = 2

GRAVITY = 9.81
TIME_STEP = 0.04
DRY_DEPTH = 0.05
SPEED_FLOOR = 0.5
BANDS = 18
ROWS = 8 * BANDS
MESH = pl.DeviceIdType.MESH


def minmod(a, b):
    return jnp.maximum(jnp.minimum(a, b), 0.0) + jnp.minimum(jnp.maximum(a, b), 0.0)


def face_sweep(own, below, slope, slope_below):
    half = [0.5 * s for s in slope]
    low = [v - s for v, s in zip(own, half)]
    high = [v + 0.5 * s for v, s in zip(below, slope_below)]

    def speeds(h, n, t):
        square = h * h
        w = 2.0 * h / (square + jnp.maximum(square, DRY_DEPTH * DRY_DEPTH))
        return w * n, w * t

    hl, nl, tl, zl = high
    hr, nr, tr, zr = low
    ul, vl = speeds(hl, nl, tl)
    ur, vr = speeds(hr, nr, tr)
    top = jnp.maximum(zl, zr)
    el = jnp.maximum(0.0, hl + zl - top)
    er = jnp.maximum(0.0, hr + zr - top)
    cl = jnp.sqrt(GRAVITY * el)
    cr = jnp.sqrt(GRAVITY * er)
    am = jnp.minimum(jnp.minimum(ul - cl, ur - cr), 0.0)
    ap = jnp.maximum(jnp.maximum(ul + cl, ur + cr), 0.0)
    inv = 1.0 / jnp.maximum(ap - am, SPEED_FLOOR)
    bp = ap * inv
    bm = am * inv
    bb = bp * am
    ml = el * ul
    mr = er * ur
    gl = 0.5 * GRAVITY * el * el
    gr = 0.5 * GRAVITY * er * er
    mass = bp * ml - bm * mr + bb * (er - el)
    push = bp * (ml * ul + gl) - bm * (mr * ur + gr) + bb * (mr - ml)
    side = bp * (ml * vl) - bm * (mr * vr) + bb * (er * vr - el * vl)
    cell_high = own[0] + half[0]
    total = hr + cell_high
    bedterm = 0.5 * GRAVITY * (total * (hr - cell_high) - 2.0 * total * half[3])
    return (mass, push + (bedterm - gr), side), (mass, push - gl, side)


def kernel(n, depth_hbm, vel_hbm, bed_hbm, lists, slots, out,
           depth, vel, bed, in_sem,
           strips, colpack, corner, rowgot, colgot, cornergot, listgot, ids,
           ext, tiles, work, mid, part, face, res,
           send_sem, recv_sem, id_sem):
    g = lax.axis_index("groups")
    r = lax.axis_index("rows")
    c = lax.axis_index("cols")
    peer = 1 - c
    half = n // 2
    shifts = (0, 1, n - 1, half, half + 1, half - 1)
    opposite = (0, 2, 1, 3, 5, 4)
    tile_cols_all = CT * 2

    def at(k, other):
        return (g, lax.rem(r + shifts[k], n), peer if other else c)

    loads = [pltpu.make_async_copy(src, dst, in_sem.at[i]) for i, (src, dst) in enumerate(
        ((depth_hbm, depth), (vel_hbm, vel), (bed_hbm, bed)))]
    for load in loads:
        load.start()
    barrier = pltpu.get_barrier_semaphore()
    for k in range(6):
        for o in range(2):
            if k or o:
                pl.semaphore_signal(barrier, inc=1, device_id=at(k, o), device_id_type=MESH)

    for load in loads:
        load.wait()
    lane8 = lax.broadcasted_iota(jnp.int32, (8, 128), 1)
    fields = (lambda rs, ls: depth[rs, ls], lambda rs, ls: vel[0, rs, ls],
              lambda rs, ls: vel[1, rs, ls], lambda rs, ls: bed[rs, ls])
    left, right, both = pl.ds(0, 128), pl.ds(128, 128), pl.ds(0, 256)
    for f in range(4):
        for e, rs in enumerate((pl.ds(0, 8), pl.ds(248, 8))):
            strips[e, f] = fields[f](rs, both)
            corner[e, f] = jnp.where(c == 0, fields[f](rs, right), fields[f](rs, left))

    @pl.loop(0, 32, unroll=8)
    def _(b):
        rs = pl.ds(pl.multiple_of(8 * b, 8), 8)
        packed = jnp.zeros((8, 128), jnp.float32)
        for f in range(4):
            slab = jnp.where(c == 0, fields[f](rs, right), fields[f](rs, left))
            packed = jnp.where(lane8 // 8 == f, pltpu.roll(slab, 4 + 8 * f, 1), packed)
        colpack[rs, :] = packed

    pl.semaphore_wait(barrier, 11)

    copies = []

    def send(src, dst, k, o):
        i = len(copies)
        copy = pltpu.make_async_remote_copy(
            src_ref=src, dst_ref=dst, send_sem=send_sem.at[i], recv_sem=recv_sem.at[i],
            device_id=at(k, o), device_id_type=MESH)
        copy.start()
        copies.append(copy)

    send(colpack, colgot, 0, 1)
    send(strips.at[1], rowgot.at[0], 1, 0)
    send(strips.at[0], rowgot.at[1], 2, 0)
    send(corner.at[1], cornergot.at[0], 1, 1)
    send(corner.at[0], cornergot.at[1], 2, 1)
    for k in (3, 0, 1, 2, 4, 5):
        for o in range(2):
            if k or o:
                send(lists, listgot.at[2 * opposite[k] + o], k, o)
    listgot[0] = lists[...]

    @pl.loop(0, 32, unroll=8)
    def _(b):
        rs = pl.ds(pl.multiple_of(8 * b, 8), 8)
        rd = pl.ds(pl.multiple_of(8 * b + 8, 8), 8)
        for j, ls in enumerate((left, right)):
            d = depth[rs, ls]
            ext[0, j, rd, :] = d
            ext[1, j, rd, :] = d * vel[0, rs, ls]
            ext[2, j, rd, :] = d * vel[1, rs, ls]
            ext[3, j, rd, :] = bed[rs, ls]

    for f in range(5):
        work[f, 0:8] = jnp.zeros((8, 256), jnp.float32)
        work[f, ROWS + 8:ROWS + 16] = jnp.zeros((8, 256), jnp.float32)
        if f < 3:
            mid[f, 0:8] = jnp.zeros((8, 256), jnp.float32)
            mid[f, ROWS + 8:ROWS + 16] = jnp.zeros((8, 256), jnp.float32)
            face[f, ROWS + 8:ROWS + 16] = jnp.zeros((8, 256), jnp.float32)

    for copy in copies:
        copy.wait_recv()
    to_ids = pltpu.make_async_copy(listgot, ids, id_sem)
    to_ids.start()

    def put(j, rd, d, a, b, z, keep):
        d = jnp.where(keep, d, 0.0)
        ext[0, j, rd, :] = d
        ext[1, j, rd, :] = d * a
        ext[2, j, rd, :] = d * b
        ext[3, j, rd, :] = jnp.where(keep, z, 0.0)

    for e, (rd, keep) in enumerate(((pl.ds(0, 8), r > 0), (pl.ds(264, 8), r < n - 1))):
        for j, ls in enumerate((left, right)):
            put(j, rd, *(rowgot[e, f, :, ls] for f in range(4)), keep)
        put(2, rd, *(cornergot[e, f] for f in range(4)), keep)

    @pl.loop(0, 32, unroll=8)
    def _(b):
        rs = pl.ds(pl.multiple_of(8 * b, 8), 8)
        rd = pl.ds(pl.multiple_of(8 * b + 8, 8), 8)
        got = colgot[rs, :]
        put(2, rd, *(pltpu.roll(got, 128 - (4 + 8 * f), 1) for f in range(4)), True)

    to_ids.wait()

    def is_active(a, b):
        row = RT * r - 1 + a
        col = CT * c - 1 + b
        inside = (row >= 0) & (row < RT * n) & (col >= 0) & (col < tile_cols_all)
        ident = row * tile_cols_all + col
        k = {0: 2, 1: 0, 2: 0, 3: 1}[a]
        o = 0 if b in (1, 2) else 1
        partner = {0: 3, 1: 4, 2: 5}[k]
        hit = ids[2 * k + o, 0, 0] == ident
        for q in (k, partner):
            for s in range(3):
                hit = hit | (ids[2 * q + o, 0, s] == ident)
        return jnp.where(hit & inside, 1.0, 0.0)

    active = [[is_active(a, b) for b in range(4)] for a in range(4)]
    lower = lane8 < 64
    at_left = (c == 0)
    for i in range(2):
        for j in range(2):
            t = 2 * i + j

            def row_of(a):
                return jnp.broadcast_to(active[a][j + 1], (8, 128)), jnp.where(
                    lower, active[a][j + 2], active[a][j])

            top, middle, bottom = row_of(i), row_of(i + 1), row_of(i + 2)

            @pl.loop(0, BANDS, unroll=6)
            def _(b):
                rs = pl.ds(pl.multiple_of(8 * b, 8), 8)
                rd = pl.ds(pl.multiple_of(8 * b + 128 * i, 8), 8)
                for f in range(4):
                    tiles[t, f, rs, 0:128] = ext[f, j, rd, :]
                    outer = ext[f, 2, rd, :]
                    inner = ext[f, 1 - j, rd, :]
                    if j == 0:
                        tiles[t, f, rs, 128:256] = jnp.where(
                            lower, inner, jnp.where(at_left, 0.0, outer))
                    else:
                        tiles[t, f, rs, 128:256] = jnp.where(
                            lower, jnp.where(at_left, outer, 0.0), inner)
                for h in range(2):
                    tiles[t, 4, rs, 128 * h:128 * h + 128] = jnp.where(
                        b == 0, top[h], jnp.where(b == BANDS - 1, bottom[h], middle[h]))

    def owned(ident):
        safe = jnp.maximum(ident, 0)
        row = lax.div(safe, tile_cols_all)
        col = lax.rem(safe, tile_cols_all)
        mine = (ident >= 0) & (lax.div(row, RT) == r) & (lax.div(col, CT) == c)
        return mine, lax.rem(row, RT) * CT + lax.rem(col, CT)

    def ranked(entries):
        first = second = count = jnp.int32(0)
        for ident in entries:
            mine, tile = owned(ident)
            first = jnp.where(mine & (count == 0), tile, first)
            second = jnp.where(mine & (count == 1), tile, second)
            count = count + jnp.where(mine, 1, 0)
        return first, second

    sent = ranked([ids[6, 0, s] for s in range(3)])
    kept = ranked([slots[s] for s in range(3)])

    row8 = lax.broadcasted_iota(jnp.int32, (8, 256), 0)

    def from_next(cur, nxt):
        edge = row8[:, :cur.shape[1]] == 7
        return jnp.where(edge, pltpu.roll(nxt, 7, 0), pltpu.roll(cur, 7, 0))

    def step(src, bed_ref):
        refs = [src.at[0], src.at[1], src.at[2], bed_ref]
        order = (0, 2, 1, 3)

        def band(b, carry):
            prev_down, prev_slope = carry
            base = pl.multiple_of(8 * b + 8, 8)
            here = pl.ds(base, 8)
            ahead = pl.ds(pl.multiple_of(8 * b + 16, 8), 8)
            v0 = [ref[here, :] for ref in refs]
            down = [pltpu.roll(v, 1, 0) for v in v0]
            vm = [jnp.where(row8 == 0, p, d) for p, d in zip(prev_down, down)]
            vp = [from_next(v, ref[ahead, :]) for v, ref in zip(v0, refs)]
            slope = [minmod(v - m, p - v) for v, m, p in zip(v0, vm, vp)]
            turned = [pltpu.roll(q, 1, 0) for q in slope]
            slope_below = [jnp.where(row8 == 0, p, d) for p, d in zip(prev_slope, turned)]
            pick = lambda vs: [vs[q] for q in order]
            gain, loss = face_sweep(pick(v0), pick(vm), pick(slope), pick(slope_below))
            for q in range(3):
                face[q, here, :] = TIME_STEP * loss[order[q]]
            left_of = [pltpu.roll(v, 1, 1) for v in v0]
            diff = [x - y for x, y in zip(v0, left_of)]
            across = [minmod(d, pltpu.roll(d, 255, 1)) for d in diff]
            across_left = [pltpu.roll(q, 1, 1) for q in across]
            xgain, xloss = face_sweep(v0, left_of, across, across_left)
            for q in range(3):
                part[q, here, :] = v0[q] + TIME_STEP * (
                    xgain[q] + gain[order[q]] - pltpu.roll(xloss[q], 255, 1))
            return down, turned

        zeros = [jnp.zeros((8, 256), jnp.float32)] * 4
        lax.fori_loop(0, BANDS, band, (zeros, zeros), unroll=6)

    def task(k, carry):
        t = jnp.where(k == 0, sent[0], jnp.where(k == 1, sent[1], jnp.where(k == 2, kept[0], kept[1])))

        @pl.loop(0, BANDS, unroll=6)
        def _(b):
            rs = pl.ds(pl.multiple_of(8 * b, 8), 8)
            rd = pl.ds(pl.multiple_of(8 * b + 8, 8), 8)
            for f in range(5):
                work[f, rd, :] = tiles[t, f, rs, :]

        step(work, work.at[3])

        @pl.loop(0, BANDS, unroll=6)
        def _(b):
            rd = pl.ds(pl.multiple_of(8 * b + 8, 8), 8)
            ahead = pl.ds(pl.multiple_of(8 * b + 16, 8), 8)
            keep = work[4, rd, :] > 0.5
            for f in range(3):
                mid[f, rd, :] = jnp.where(
                    keep, part[f, rd, :] - from_next(face[f, rd, :], face[f, ahead, :]), work[f, rd, :])

        step(mid, work.at[3])

        @pl.loop(0, 16, unroll=8)
        def _(b):
            rd = pl.ds(pl.multiple_of(8 * b + 16, 8), 8)
            ahead = pl.ds(pl.multiple_of(8 * b + 24, 8), 8)
            for f in range(3):
                res[k, f, pl.ds(pl.multiple_of(8 * b, 8), 8), :] = (
                    part[f, rd, 0:128] - from_next(face[f, rd, 0:128], face[f, ahead, 0:128]))

        @pl.when(k < 2)
        def _():
            result_copy(k).start()

        return carry

    def result_copy(k):
        return pltpu.make_async_remote_copy(
            src_ref=res.at[k], dst_ref=res.at[4 + k], send_sem=send_sem.at[16 + k],
            recv_sem=recv_sem.at[16 + k], device_id=at(3, 0), device_id_type=MESH)

    lax.fori_loop(0, 4, task, 0)
    for k in range(2):
        result_copy(k).wait_recv()

    own_rank = far_rank = jnp.int32(0)
    for s in range(3):
        ident = slots[s]
        mine, _ = owned(ident)
        far = (ident >= 0) & jnp.logical_not(mine)
        index = jnp.where(mine, 2 + own_rank, jnp.where(far, 4 + far_rank, 2))
        index = jnp.minimum(index, 5)
        own_rank = own_rank + jnp.where(mine, 1, 0)
        far_rank = far_rank + jnp.where(far, 1, 0)

        @pl.loop(0, 16, unroll=8)
        def _(b):
            rs = pl.ds(pl.multiple_of(8 * b, 8), 8)
            for f in range(3):
                out[0, 0, s, f, rs, :] = jnp.where(ident >= 0, res[index, f, rs, :], 0.0)

    for copy in copies:
        copy.wait_send()
    for k in range(2):
        result_copy(k).wait_send()


def shards(depth, velocity, bed, slots):
    n = lax.axis_size("rows")
    listed = slots[0, 0]
    lists = jnp.pad(listed[None, :], ((0, 0), (0, 125)), constant_values=-1)
    vmem = pl.BlockSpec(memory_space=pltpu.VMEM)
    f32 = jnp.float32
    return pl.pallas_call(
        functools.partial(kernel, n),
        out_shape=jax.ShapeDtypeStruct((1, 1, 3, 3, TILE, TILE), f32),
        in_specs=[pl.BlockSpec(memory_space=pltpu.HBM)] * 3 + [vmem] + [pl.BlockSpec(memory_space=pltpu.SMEM)],
        out_specs=vmem,
        scratch_shapes=[
            pltpu.VMEM((256, 256), f32),
            pltpu.VMEM((2, 256, 256), f32),
            pltpu.VMEM((256, 256), f32),
            pltpu.SemaphoreType.DMA((3,)),
            pltpu.VMEM((2, 4, 8, 256), f32),
            pltpu.VMEM((256, 128), f32),
            pltpu.VMEM((2, 4, 8, 128), f32),
            pltpu.VMEM((2, 4, 8, 256), f32),
            pltpu.VMEM((256, 128), f32),
            pltpu.VMEM((2, 4, 8, 128), f32),
            pltpu.VMEM((12, 1, 128), jnp.int32),
            pltpu.SMEM((12, 1, 128), jnp.int32),
            pltpu.VMEM((4, 3, 272, 128), f32),
            pltpu.VMEM((4, 5, ROWS, 256), f32),
            pltpu.VMEM((5, ROWS + 16, 256), f32),
            pltpu.VMEM((3, ROWS + 16, 256), f32),
            pltpu.VMEM((3, ROWS + 16, 256), f32),
            pltpu.VMEM((3, ROWS + 16, 256), f32),
            pltpu.VMEM((6, 3, TILE, TILE), f32),
            pltpu.SemaphoreType.DMA((18,)),
            pltpu.SemaphoreType.DMA((18,)),
            pltpu.SemaphoreType.DMA,
        ],
        compiler_params=pltpu.CompilerParams(
            collective_id=0, has_side_effects=True, vmem_limit_bytes=40 * 2**20),
    )(depth, velocity, bed, lists, listed)


def solution(mesh):
    in_specs = (
        P(("groups", "rows"), "cols"),
        P(None, ("groups", "rows"), "cols"),
        P(("groups", "rows"), "cols"),
        P(("groups", "rows"), "cols", None),
    )
    out_specs = P(("groups", "rows"), "cols", None, None, None, None)
    return jax.shard_map(shards, mesh=mesh, in_specs=in_specs, out_specs=out_specs, check_vma=False)
```

```python
import functools

import jax
import jax.numpy as jnp
from jax import lax
from jax.experimental import pallas as pl
from jax.experimental.pallas import tpu as pltpu
from jax.sharding import PartitionSpec as P

TILE = 128
RT = 2
CT = 2

GRAVITY = 9.81
TIME_STEP = 0.04
DRY_DEPTH = 0.05
SPEED_FLOOR = 0.5
BANDS = 18
PART_ROWS = 64
PART_BANDS = 10
ROWS = 8 * PART_BANDS
VMEM_LIMIT = 63 * 2**20
MESH = pl.DeviceIdType.MESH


def minmod(a, b):
    return jnp.maximum(jnp.minimum(a, b), 0.0) + jnp.minimum(jnp.maximum(a, b), 0.0)


def face_sweep(own, below, slope, slope_below):
    half = [0.5 * s for s in slope]
    low = [v - s for v, s in zip(own, half)]
    high = [v + 0.5 * s for v, s in zip(below, slope_below)]

    def speeds(h, n, t):
        square = h * h
        w = 2.0 * h / (square + jnp.maximum(square, DRY_DEPTH * DRY_DEPTH))
        return w * n, w * t

    hl, nl, tl, zl = high
    hr, nr, tr, zr = low
    ul, vl = speeds(hl, nl, tl)
    ur, vr = speeds(hr, nr, tr)
    top = jnp.maximum(zl, zr)
    el = jnp.maximum(0.0, hl + zl - top)
    er = jnp.maximum(0.0, hr + zr - top)
    cl = jnp.sqrt(GRAVITY * el)
    cr = jnp.sqrt(GRAVITY * er)
    am = jnp.minimum(jnp.minimum(ul - cl, ur - cr), 0.0)
    ap = jnp.maximum(jnp.maximum(ul + cl, ur + cr), 0.0)
    inv = 1.0 / jnp.maximum(ap - am, SPEED_FLOOR)
    bp = ap * inv
    bm = am * inv
    bb = bp * am
    ml = el * ul
    mr = er * ur
    gl = 0.5 * GRAVITY * el * el
    gr = 0.5 * GRAVITY * er * er
    mass = bp * ml - bm * mr + bb * (er - el)
    push = bp * (ml * ul + gl) - bm * (mr * ur + gr) + bb * (mr - ml)
    side = bp * (ml * vl) - bm * (mr * vr) + bb * (er * vr - el * vl)
    cell_high = own[0] + half[0]
    total = hr + cell_high
    bedterm = 0.5 * GRAVITY * (total * (hr - cell_high) - 2.0 * total * half[3])
    return (mass, push + (bedterm - gr), side), (mass, push - gl, side)


def kernel(n, depth_hbm, vel_hbm, bed_hbm, slots, out,
           depth, vel, bed, in_sem, lists,
           strips, colpack, corner, rowgot, colgot, cornergot, listgot, ids,
           ext, tiles, work, mid, part, face, res,
           send_sem, recv_sem, id_sem):
    g = lax.axis_index("groups")
    r = lax.axis_index("rows")
    c = lax.axis_index("cols")
    peer = 1 - c
    half = n // 2
    shifts = (0, 1, n - 1, half, half + 1, half - 1)
    opposite = (0, 2, 1, 3, 5, 4)
    tile_cols_all = CT * 2

    def at(k, other):
        return (g, lax.rem(r + shifts[k], n), peer if other else c)

    loads = [pltpu.make_async_copy(src, dst, in_sem.at[i]) for i, (src, dst) in enumerate(
        ((depth_hbm, depth), (vel_hbm, vel), (bed_hbm, bed)))]
    for load in loads:
        load.start()
    place = lax.broadcasted_iota(jnp.int32, (1, 128), 1)
    lists[...] = jnp.where(place == 0, slots[0], jnp.where(
        place == 1, slots[1], jnp.where(place == 2, slots[2], -1)))
    barrier = pltpu.get_barrier_semaphore()
    for k in range(6):
        for o in range(2):
            if k or o:
                pl.semaphore_signal(barrier, inc=1, device_id=at(k, o), device_id_type=MESH)

    for load in loads:
        load.wait()
    lane8 = lax.broadcasted_iota(jnp.int32, (8, 128), 1)
    fields = (lambda rs, ls: depth[rs, ls], lambda rs, ls: vel[0, rs, ls],
              lambda rs, ls: vel[1, rs, ls], lambda rs, ls: bed[rs, ls])
    left, right, both = pl.ds(0, 128), pl.ds(128, 128), pl.ds(0, 256)
    for f in range(4):
        for e, rs in enumerate((pl.ds(0, 8), pl.ds(248, 8))):
            strips[e, f] = fields[f](rs, both)
            corner[e, f] = jnp.where(c == 0, fields[f](rs, right), fields[f](rs, left))

    @pl.loop(0, 32, unroll=8)
    def _(b):
        rs = pl.ds(pl.multiple_of(8 * b, 8), 8)
        packed = jnp.zeros((8, 128), jnp.float32)
        for f in range(4):
            slab = jnp.where(c == 0, fields[f](rs, right), fields[f](rs, left))
            packed = jnp.where(lane8 // 8 == f, pltpu.roll(slab, 4 + 8 * f, 1), packed)
        colpack[rs, :] = packed

    pl.semaphore_wait(barrier, 11)

    copies = []

    def send(src, dst, k, o):
        i = len(copies)
        copy = pltpu.make_async_remote_copy(
            src_ref=src, dst_ref=dst, send_sem=send_sem.at[i], recv_sem=recv_sem.at[i],
            device_id=at(k, o), device_id_type=MESH)
        copy.start()
        copies.append(copy)

    send(colpack, colgot, 0, 1)
    send(strips.at[1], rowgot.at[0], 1, 0)
    send(strips.at[0], rowgot.at[1], 2, 0)
    send(corner.at[1], cornergot.at[0], 1, 1)
    send(corner.at[0], cornergot.at[1], 2, 1)
    for k in (3, 0, 1, 2, 4, 5):
        for o in range(2):
            if k or o:
                send(lists, listgot.at[2 * opposite[k] + o], k, o)
    listgot[0] = lists[...]

    @pl.loop(0, 32, unroll=8)
    def _(b):
        rs = pl.ds(pl.multiple_of(8 * b, 8), 8)
        rd = pl.ds(pl.multiple_of(8 * b + 8, 8), 8)
        for j, ls in enumerate((left, right)):
            d = depth[rs, ls]
            ext[0, j, rd, :] = d
            ext[1, j, rd, :] = d * vel[0, rs, ls]
            ext[2, j, rd, :] = d * vel[1, rs, ls]
            ext[3, j, rd, :] = bed[rs, ls]

    for f in range(5):
        work[f, 0:8] = jnp.zeros((8, 256), jnp.float32)
        work[f, ROWS + 8:ROWS + 16] = jnp.zeros((8, 256), jnp.float32)
        if f < 3:
            mid[f, 0:8] = jnp.zeros((8, 256), jnp.float32)
            mid[f, ROWS + 8:ROWS + 16] = jnp.zeros((8, 256), jnp.float32)
            face[f, ROWS + 8:ROWS + 16] = jnp.zeros((8, 256), jnp.float32)

    for copy in copies:
        copy.wait_recv()
    to_ids = pltpu.make_async_copy(listgot, ids, id_sem)
    to_ids.start()

    def put(j, rd, d, a, b, z, keep):
        d = jnp.where(keep, d, 0.0)
        ext[0, j, rd, :] = d
        ext[1, j, rd, :] = d * a
        ext[2, j, rd, :] = d * b
        ext[3, j, rd, :] = jnp.where(keep, z, 0.0)

    for e, (rd, keep) in enumerate(((pl.ds(0, 8), r > 0), (pl.ds(264, 8), r < n - 1))):
        for j, ls in enumerate((left, right)):
            put(j, rd, *(rowgot[e, f, :, ls] for f in range(4)), keep)
        put(2, rd, *(cornergot[e, f] for f in range(4)), keep)

    @pl.loop(0, 32, unroll=8)
    def _(b):
        rs = pl.ds(pl.multiple_of(8 * b, 8), 8)
        rd = pl.ds(pl.multiple_of(8 * b + 8, 8), 8)
        got = colgot[rs, :]
        put(2, rd, *(pltpu.roll(got, 128 - (4 + 8 * f), 1) for f in range(4)), True)

    to_ids.wait()

    def is_active(a, b):
        row = RT * r - 1 + a
        col = CT * c - 1 + b
        inside = (row >= 0) & (row < RT * n) & (col >= 0) & (col < tile_cols_all)
        ident = row * tile_cols_all + col
        k = {0: 2, 1: 0, 2: 0, 3: 1}[a]
        o = 0 if b in (1, 2) else 1
        partner = {0: 3, 1: 4, 2: 5}[k]
        hit = ids[2 * k + o, 0, 0] == ident
        for q in (k, partner):
            for s in range(3):
                hit = hit | (ids[2 * q + o, 0, s] == ident)
        return jnp.where(hit & inside, 1.0, 0.0)

    active = [[is_active(a, b) for b in range(4)] for a in range(4)]
    lower = lane8 < 64
    at_left = (c == 0)
    for i in range(2):
        for j in range(2):
            t = 2 * i + j

            def row_of(a):
                return jnp.broadcast_to(active[a][j + 1], (8, 128)), jnp.where(
                    lower, active[a][j + 2], active[a][j])

            top, middle, bottom = row_of(i), row_of(i + 1), row_of(i + 2)

            @pl.loop(0, BANDS, unroll=6)
            def _(b):
                rs = pl.ds(pl.multiple_of(8 * b, 8), 8)
                rd = pl.ds(pl.multiple_of(8 * b + 128 * i, 8), 8)
                for f in range(4):
                    tiles[t, f, rs, 0:128] = ext[f, j, rd, :]
                    outer = ext[f, 2, rd, :]
                    inner = ext[f, 1 - j, rd, :]
                    if j == 0:
                        tiles[t, f, rs, 128:256] = jnp.where(
                            lower, inner, jnp.where(at_left, 0.0, outer))
                    else:
                        tiles[t, f, rs, 128:256] = jnp.where(
                            lower, jnp.where(at_left, outer, 0.0), inner)
                for h in range(2):
                    tiles[t, 4, rs, 128 * h:128 * h + 128] = jnp.where(
                        b == 0, top[h], jnp.where(b == BANDS - 1, bottom[h], middle[h]))

    def owned(ident):
        safe = jnp.maximum(ident, 0)
        row = lax.div(safe, tile_cols_all)
        col = lax.rem(safe, tile_cols_all)
        mine = (ident >= 0) & (lax.div(row, RT) == r) & (lax.div(col, CT) == c)
        return mine, lax.rem(row, RT) * CT + lax.rem(col, CT)

    def ranked(entries):
        first = second = count = jnp.int32(0)
        for ident in entries:
            mine, tile = owned(ident)
            first = jnp.where(mine & (count == 0), tile, first)
            second = jnp.where(mine & (count == 1), tile, second)
            count = count + jnp.where(mine, 1, 0)
        return first, second

    sent = ranked([ids[6, 0, s] for s in range(3)])
    kept = ranked([slots[s] for s in range(3)])

    row8 = lax.broadcasted_iota(jnp.int32, (8, 256), 0)

    def from_next(cur, nxt):
        edge = row8[:, :cur.shape[1]] == 7
        return jnp.where(edge, pltpu.roll(nxt, 7, 0), pltpu.roll(cur, 7, 0))

    def step(src, bed_ref):
        refs = [src.at[0], src.at[1], src.at[2], bed_ref]
        order = (0, 2, 1, 3)

        def band(b, carry):
            prev_down, prev_slope = carry
            base = pl.multiple_of(8 * b + 8, 8)
            here = pl.ds(base, 8)
            ahead = pl.ds(pl.multiple_of(8 * b + 16, 8), 8)
            v0 = [ref[here, :] for ref in refs]
            down = [pltpu.roll(v, 1, 0) for v in v0]
            vm = [jnp.where(row8 == 0, p, d) for p, d in zip(prev_down, down)]
            vp = [from_next(v, ref[ahead, :]) for v, ref in zip(v0, refs)]
            slope = [minmod(v - m, p - v) for v, m, p in zip(v0, vm, vp)]
            turned = [pltpu.roll(q, 1, 0) for q in slope]
            slope_below = [jnp.where(row8 == 0, p, d) for p, d in zip(prev_slope, turned)]
            pick = lambda vs: [vs[q] for q in order]
            gain, loss = face_sweep(pick(v0), pick(vm), pick(slope), pick(slope_below))
            for q in range(3):
                face[q, here, :] = TIME_STEP * loss[order[q]]
            left_of = [pltpu.roll(v, 1, 1) for v in v0]
            diff = [x - y for x, y in zip(v0, left_of)]
            across = [minmod(d, pltpu.roll(d, 255, 1)) for d in diff]
            across_left = [pltpu.roll(q, 1, 1) for q in across]
            xgain, xloss = face_sweep(v0, left_of, across, across_left)
            for q in range(3):
                part[q, here, :] = v0[q] + TIME_STEP * (
                    xgain[q] + gain[order[q]] - pltpu.roll(xloss[q], 255, 1))
            return down, turned

        zeros = [jnp.zeros((8, 256), jnp.float32)] * 4
        lax.fori_loop(0, PART_BANDS, band, (zeros, zeros), unroll=10)

    def task(q, carry):
        k = lax.div(q, 2)
        first = PART_ROWS * lax.rem(q, 2)
        t = jnp.where(k == 0, sent[0], jnp.where(k == 1, sent[1], jnp.where(k == 2, kept[0], kept[1])))

        @pl.loop(0, PART_BANDS, unroll=5)
        def _(b):
            rs = pl.ds(pl.multiple_of(first + 8 * b, 8), 8)
            rd = pl.ds(pl.multiple_of(8 * b + 8, 8), 8)
            for f in range(5):
                work[f, rd, :] = tiles[t, f, rs, :]

        step(work, work.at[3])

        @pl.loop(0, PART_BANDS, unroll=5)
        def _(b):
            rd = pl.ds(pl.multiple_of(8 * b + 8, 8), 8)
            ahead = pl.ds(pl.multiple_of(8 * b + 16, 8), 8)
            keep = work[4, rd, :] > 0.5
            for f in range(3):
                mid[f, rd, :] = jnp.where(
                    keep, part[f, rd, :] - from_next(face[f, rd, :], face[f, ahead, :]), work[f, rd, :])

        step(mid, work.at[3])

        @pl.loop(0, 8, unroll=8)
        def _(b):
            rd = pl.ds(pl.multiple_of(8 * b + 16, 8), 8)
            ahead = pl.ds(pl.multiple_of(8 * b + 24, 8), 8)
            for f in range(3):
                res[k, f, pl.ds(pl.multiple_of(first + 8 * b, 8), 8), :] = (
                    part[f, rd, 0:128] - from_next(face[f, rd, 0:128], face[f, ahead, 0:128]))

        @pl.when(q < 4)
        def _():
            result_copy(q).start()

        return carry

    def result_copy(q):
        k = lax.div(q, 2) if not isinstance(q, int) else q // 2
        first = pl.multiple_of(PART_ROWS * (lax.rem(q, 2) if not isinstance(q, int) else q % 2), 8)
        rows = pl.ds(first, PART_ROWS)
        return pltpu.make_async_remote_copy(
            src_ref=res.at[k, :, rows, :], dst_ref=res.at[4 + k, :, rows, :], send_sem=send_sem.at[16 + q],
            recv_sem=recv_sem.at[16 + q], device_id=at(3, 0), device_id_type=MESH)

    lax.fori_loop(0, 8, task, 0)
    for q in range(4):
        result_copy(q).wait_recv()

    own_rank = far_rank = jnp.int32(0)
    for s in range(3):
        ident = slots[s]
        mine, _ = owned(ident)
        far = (ident >= 0) & jnp.logical_not(mine)
        index = jnp.where(mine, 2 + own_rank, jnp.where(far, 4 + far_rank, 2))
        index = jnp.minimum(index, 5)
        own_rank = own_rank + jnp.where(mine, 1, 0)
        far_rank = far_rank + jnp.where(far, 1, 0)

        @pl.loop(0, 16, unroll=8)
        def _(b):
            rs = pl.ds(pl.multiple_of(8 * b, 8), 8)
            for f in range(3):
                out[0, 0, s, f, rs, :] = jnp.where(ident >= 0, res[index, f, rs, :], 0.0)

    for copy in copies:
        copy.wait_send()
    for q in range(4):
        result_copy(q).wait_send()


def shards(depth, velocity, bed, slots):
    n = lax.axis_size("rows")
    listed = slots[0, 0]
    vmem = pl.BlockSpec(memory_space=pltpu.VMEM)
    f32 = jnp.float32
    return pl.pallas_call(
        functools.partial(kernel, n),
        out_shape=jax.ShapeDtypeStruct((1, 1, 3, 3, TILE, TILE), f32),
        in_specs=[pl.BlockSpec(memory_space=pltpu.HBM)] * 3 + [pl.BlockSpec(memory_space=pltpu.SMEM)],
        out_specs=vmem,
        scratch_shapes=[
            pltpu.VMEM((256, 256), f32),
            pltpu.VMEM((2, 256, 256), f32),
            pltpu.VMEM((256, 256), f32),
            pltpu.SemaphoreType.DMA((3,)),
            pltpu.VMEM((1, 128), jnp.int32),
            pltpu.VMEM((2, 4, 8, 256), f32),
            pltpu.VMEM((256, 128), f32),
            pltpu.VMEM((2, 4, 8, 128), f32),
            pltpu.VMEM((2, 4, 8, 256), f32),
            pltpu.VMEM((256, 128), f32),
            pltpu.VMEM((2, 4, 8, 128), f32),
            pltpu.VMEM((12, 1, 128), jnp.int32),
            pltpu.SMEM((12, 1, 128), jnp.int32),
            pltpu.VMEM((4, 3, 272, 128), f32),
            pltpu.VMEM((4, 5, 8 * BANDS, 256), f32),
            pltpu.VMEM((5, ROWS + 16, 256), f32),
            pltpu.VMEM((3, ROWS + 16, 256), f32),
            pltpu.VMEM((3, ROWS + 16, 256), f32),
            pltpu.VMEM((3, ROWS + 16, 256), f32),
            pltpu.VMEM((6, 3, TILE, TILE), f32),
            pltpu.SemaphoreType.DMA((20,)),
            pltpu.SemaphoreType.DMA((20,)),
            pltpu.SemaphoreType.DMA,
        ],
        compiler_params=pltpu.CompilerParams(
            collective_id=0, has_side_effects=True, vmem_limit_bytes=VMEM_LIMIT),
    )(depth, velocity, bed, listed)


def solution(mesh):
    in_specs = (
        P(("groups", "rows"), "cols"),
        P(None, ("groups", "rows"), "cols"),
        P(("groups", "rows"), "cols"),
        P(("groups", "rows"), "cols", None),
    )
    out_specs = P(("groups", "rows"), "cols", None, None, None, None)
    return jax.shard_map(shards, mesh=mesh, in_specs=in_specs, out_specs=out_specs, check_vma=False)
```

```python
import functools

import jax
import jax.numpy as jnp
from jax import lax
from jax.experimental import pallas as pl
from jax.experimental.pallas import tpu as pltpu
from jax.sharding import PartitionSpec as P

TILE = 128
RT = 2
CT = 2

GRAVITY = 9.81
TIME_STEP = 0.04
DRY_DEPTH = 0.05
SPEED_FLOOR = 0.5
BANDS = 18
PART_ROWS = 32
PART_BANDS = 6
ROWS = 8 * PART_BANDS
VMEM_LIMIT = 63 * 2**20
MESH = pl.DeviceIdType.MESH


def minmod(a, b):
    return jnp.maximum(jnp.minimum(a, b), 0.0) + jnp.minimum(jnp.maximum(a, b), 0.0)


def face_sweep(own, below, slope, slope_below):
    half = [0.5 * s for s in slope]
    low = [v - s for v, s in zip(own, half)]
    high = [v + 0.5 * s for v, s in zip(below, slope_below)]

    def speeds(h, n, t):
        square = h * h
        w = 2.0 * h / (square + jnp.maximum(square, DRY_DEPTH * DRY_DEPTH))
        return w * n, w * t

    hl, nl, tl, zl = high
    hr, nr, tr, zr = low
    ul, vl = speeds(hl, nl, tl)
    ur, vr = speeds(hr, nr, tr)
    top = jnp.maximum(zl, zr)
    el = jnp.maximum(0.0, hl + zl - top)
    er = jnp.maximum(0.0, hr + zr - top)
    cl = jnp.sqrt(GRAVITY * el)
    cr = jnp.sqrt(GRAVITY * er)
    am = jnp.minimum(jnp.minimum(ul - cl, ur - cr), 0.0)
    ap = jnp.maximum(jnp.maximum(ul + cl, ur + cr), 0.0)
    inv = 1.0 / jnp.maximum(ap - am, SPEED_FLOOR)
    bp = ap * inv
    bm = am * inv
    bb = bp * am
    ml = el * ul
    mr = er * ur
    gl = 0.5 * GRAVITY * el * el
    gr = 0.5 * GRAVITY * er * er
    mass = bp * ml - bm * mr + bb * (er - el)
    push = bp * (ml * ul + gl) - bm * (mr * ur + gr) + bb * (mr - ml)
    side = bp * (ml * vl) - bm * (mr * vr) + bb * (er * vr - el * vl)
    cell_high = own[0] + half[0]
    total = hr + cell_high
    bedterm = 0.5 * GRAVITY * (total * (hr - cell_high) - 2.0 * total * half[3])
    return (mass, push + (bedterm - gr), side), (mass, push - gl, side)


def kernel(n, depth_hbm, vel_hbm, bed_hbm, slots, out,
           depth, vel, bed, in_sem, lists,
           strips, colpack, corner, rowgot, colgot, cornergot, listgot, ids,
           ext, tiles, work, mid, part, face, res,
           send_sem, recv_sem, id_sem):
    g = lax.axis_index("groups")
    r = lax.axis_index("rows")
    c = lax.axis_index("cols")
    peer = 1 - c
    half = n // 2
    shifts = (0, 1, n - 1, half, half + 1, half - 1)
    opposite = (0, 2, 1, 3, 5, 4)
    tile_cols_all = CT * 2

    def at(k, other):
        return (g, lax.rem(r + shifts[k], n), peer if other else c)

    loads = [pltpu.make_async_copy(src, dst, in_sem.at[i]) for i, (src, dst) in enumerate(
        ((depth_hbm, depth), (vel_hbm, vel), (bed_hbm, bed)))]
    for load in loads:
        load.start()
    place = lax.broadcasted_iota(jnp.int32, (1, 128), 1)
    lists[...] = jnp.where(place == 0, slots[0], jnp.where(
        place == 1, slots[1], jnp.where(place == 2, slots[2], -1)))
    barrier = pltpu.get_barrier_semaphore()
    for k in range(6):
        for o in range(2):
            if k or o:
                pl.semaphore_signal(barrier, inc=1, device_id=at(k, o), device_id_type=MESH)

    for load in loads:
        load.wait()
    lane8 = lax.broadcasted_iota(jnp.int32, (8, 128), 1)
    fields = (lambda rs, ls: depth[rs, ls], lambda rs, ls: vel[0, rs, ls],
              lambda rs, ls: vel[1, rs, ls], lambda rs, ls: bed[rs, ls])
    left, right, both = pl.ds(0, 128), pl.ds(128, 128), pl.ds(0, 256)
    for f in range(4):
        for e, rs in enumerate((pl.ds(0, 8), pl.ds(248, 8))):
            strips[e, f] = fields[f](rs, both)
            corner[e, f] = jnp.where(c == 0, fields[f](rs, right), fields[f](rs, left))

    @pl.loop(0, 32, unroll=8)
    def _(b):
        rs = pl.ds(pl.multiple_of(8 * b, 8), 8)
        packed = jnp.zeros((8, 128), jnp.float32)
        for f in range(4):
            slab = jnp.where(c == 0, fields[f](rs, right), fields[f](rs, left))
            packed = jnp.where(lane8 // 8 == f, pltpu.roll(slab, 4 + 8 * f, 1), packed)
        colpack[rs, :] = packed

    pl.semaphore_wait(barrier, 11)

    copies = []

    def send(src, dst, k, o):
        i = len(copies)
        copy = pltpu.make_async_remote_copy(
            src_ref=src, dst_ref=dst, send_sem=send_sem.at[i], recv_sem=recv_sem.at[i],
            device_id=at(k, o), device_id_type=MESH)
        copy.start()
        copies.append(copy)

    send(colpack, colgot, 0, 1)
    send(strips.at[1], rowgot.at[0], 1, 0)
    send(strips.at[0], rowgot.at[1], 2, 0)
    send(corner.at[1], cornergot.at[0], 1, 1)
    send(corner.at[0], cornergot.at[1], 2, 1)
    for k in (3, 0, 1, 2, 4, 5):
        for o in range(2):
            if k or o:
                send(lists, listgot.at[2 * opposite[k] + o], k, o)
    listgot[0] = lists[...]

    @pl.loop(0, 32, unroll=8)
    def _(b):
        rs = pl.ds(pl.multiple_of(8 * b, 8), 8)
        rd = pl.ds(pl.multiple_of(8 * b + 8, 8), 8)
        for j, ls in enumerate((left, right)):
            d = depth[rs, ls]
            ext[0, j, rd, :] = d
            ext[1, j, rd, :] = d * vel[0, rs, ls]
            ext[2, j, rd, :] = d * vel[1, rs, ls]
            ext[3, j, rd, :] = bed[rs, ls]

    for f in range(5):
        work[f, 0:8] = jnp.zeros((8, 256), jnp.float32)
        work[f, ROWS + 8:ROWS + 16] = jnp.zeros((8, 256), jnp.float32)
        if f < 3:
            mid[f, 0:8] = jnp.zeros((8, 256), jnp.float32)
            mid[f, ROWS + 8:ROWS + 16] = jnp.zeros((8, 256), jnp.float32)
            face[f, ROWS + 8:ROWS + 16] = jnp.zeros((8, 256), jnp.float32)

    for copy in copies:
        copy.wait_recv()
    to_ids = pltpu.make_async_copy(listgot, ids, id_sem)
    to_ids.start()

    def put(j, rd, d, a, b, z, keep):
        d = jnp.where(keep, d, 0.0)
        ext[0, j, rd, :] = d
        ext[1, j, rd, :] = d * a
        ext[2, j, rd, :] = d * b
        ext[3, j, rd, :] = jnp.where(keep, z, 0.0)

    for e, (rd, keep) in enumerate(((pl.ds(0, 8), r > 0), (pl.ds(264, 8), r < n - 1))):
        for j, ls in enumerate((left, right)):
            put(j, rd, *(rowgot[e, f, :, ls] for f in range(4)), keep)
        put(2, rd, *(cornergot[e, f] for f in range(4)), keep)

    @pl.loop(0, 32, unroll=8)
    def _(b):
        rs = pl.ds(pl.multiple_of(8 * b, 8), 8)
        rd = pl.ds(pl.multiple_of(8 * b + 8, 8), 8)
        got = colgot[rs, :]
        put(2, rd, *(pltpu.roll(got, 128 - (4 + 8 * f), 1) for f in range(4)), True)

    to_ids.wait()

    def is_active(a, b):
        row = RT * r - 1 + a
        col = CT * c - 1 + b
        inside = (row >= 0) & (row < RT * n) & (col >= 0) & (col < tile_cols_all)
        ident = row * tile_cols_all + col
        k = {0: 2, 1: 0, 2: 0, 3: 1}[a]
        o = 0 if b in (1, 2) else 1
        partner = {0: 3, 1: 4, 2: 5}[k]
        hit = ids[2 * k + o, 0, 0] == ident
        for q in (k, partner):
            for s in range(3):
                hit = hit | (ids[2 * q + o, 0, s] == ident)
        return jnp.where(hit & inside, 1.0, 0.0)

    active = [[is_active(a, b) for b in range(4)] for a in range(4)]
    lower = lane8 < 64
    at_left = (c == 0)
    for i in range(2):
        for j in range(2):
            t = 2 * i + j

            def row_of(a):
                return jnp.broadcast_to(active[a][j + 1], (8, 128)), jnp.where(
                    lower, active[a][j + 2], active[a][j])

            top, middle, bottom = row_of(i), row_of(i + 1), row_of(i + 2)

            @pl.loop(0, BANDS, unroll=6)
            def _(b):
                rs = pl.ds(pl.multiple_of(8 * b, 8), 8)
                rd = pl.ds(pl.multiple_of(8 * b + 128 * i, 8), 8)
                for f in range(4):
                    tiles[t, f, rs, 0:128] = ext[f, j, rd, :]
                    outer = ext[f, 2, rd, :]
                    inner = ext[f, 1 - j, rd, :]
                    if j == 0:
                        tiles[t, f, rs, 128:256] = jnp.where(
                            lower, inner, jnp.where(at_left, 0.0, outer))
                    else:
                        tiles[t, f, rs, 128:256] = jnp.where(
                            lower, jnp.where(at_left, outer, 0.0), inner)
                for h in range(2):
                    tiles[t, 4, rs, 128 * h:128 * h + 128] = jnp.where(
                        b == 0, top[h], jnp.where(b == BANDS - 1, bottom[h], middle[h]))

    def owned(ident):
        safe = jnp.maximum(ident, 0)
        row = lax.div(safe, tile_cols_all)
        col = lax.rem(safe, tile_cols_all)
        mine = (ident >= 0) & (lax.div(row, RT) == r) & (lax.div(col, CT) == c)
        return mine, lax.rem(row, RT) * CT + lax.rem(col, CT)

    def ranked(entries):
        first = second = count = jnp.int32(0)
        for ident in entries:
            mine, tile = owned(ident)
            first = jnp.where(mine & (count == 0), tile, first)
            second = jnp.where(mine & (count == 1), tile, second)
            count = count + jnp.where(mine, 1, 0)
        return first, second

    sent = ranked([ids[6, 0, s] for s in range(3)])
    kept = ranked([slots[s] for s in range(3)])

    row8 = lax.broadcasted_iota(jnp.int32, (8, 256), 0)

    def from_next(cur, nxt):
        edge = row8[:, :cur.shape[1]] == 7
        return jnp.where(edge, pltpu.roll(nxt, 7, 0), pltpu.roll(cur, 7, 0))

    def step(src, bed_ref):
        refs = [src.at[0], src.at[1], src.at[2], bed_ref]
        order = (0, 2, 1, 3)

        def band(b, carry):
            prev_down, prev_slope = carry
            base = pl.multiple_of(8 * b + 8, 8)
            here = pl.ds(base, 8)
            ahead = pl.ds(pl.multiple_of(8 * b + 16, 8), 8)
            v0 = [ref[here, :] for ref in refs]
            down = [pltpu.roll(v, 1, 0) for v in v0]
            vm = [jnp.where(row8 == 0, p, d) for p, d in zip(prev_down, down)]
            vp = [from_next(v, ref[ahead, :]) for v, ref in zip(v0, refs)]
            slope = [minmod(v - m, p - v) for v, m, p in zip(v0, vm, vp)]
            turned = [pltpu.roll(q, 1, 0) for q in slope]
            slope_below = [jnp.where(row8 == 0, p, d) for p, d in zip(prev_slope, turned)]
            pick = lambda vs: [vs[q] for q in order]
            gain, loss = face_sweep(pick(v0), pick(vm), pick(slope), pick(slope_below))
            for q in range(3):
                face[q, here, :] = TIME_STEP * loss[order[q]]
            left_of = [pltpu.roll(v, 1, 1) for v in v0]
            diff = [x - y for x, y in zip(v0, left_of)]
            across = [minmod(d, pltpu.roll(d, 255, 1)) for d in diff]
            across_left = [pltpu.roll(q, 1, 1) for q in across]
            xgain, xloss = face_sweep(v0, left_of, across, across_left)
            for q in range(3):
                part[q, here, :] = v0[q] + TIME_STEP * (
                    xgain[q] + gain[order[q]] - pltpu.roll(xloss[q], 255, 1))
            return down, turned

        zeros = [jnp.zeros((8, 256), jnp.float32)] * 4
        lax.fori_loop(0, PART_BANDS, band, (zeros, zeros), unroll=6)

    def task(q, carry):
        k = lax.div(q, 4)
        first = PART_ROWS * lax.rem(q, 4)
        t = jnp.where(k == 0, sent[0], jnp.where(k == 1, sent[1], jnp.where(k == 2, kept[0], kept[1])))

        @pl.loop(0, PART_BANDS, unroll=6)
        def _(b):
            rs = pl.ds(pl.multiple_of(first + 8 * b, 8), 8)
            rd = pl.ds(pl.multiple_of(8 * b + 8, 8), 8)
            for f in range(5):
                work[f, rd, :] = tiles[t, f, rs, :]

        step(work, work.at[3])

        @pl.loop(0, PART_BANDS, unroll=6)
        def _(b):
            rd = pl.ds(pl.multiple_of(8 * b + 8, 8), 8)
            ahead = pl.ds(pl.multiple_of(8 * b + 16, 8), 8)
            keep = work[4, rd, :] > 0.5
            for f in range(3):
                mid[f, rd, :] = jnp.where(
                    keep, part[f, rd, :] - from_next(face[f, rd, :], face[f, ahead, :]), work[f, rd, :])

        step(mid, work.at[3])

        @pl.loop(0, 4, unroll=4)
        def _(b):
            rd = pl.ds(pl.multiple_of(8 * b + 16, 8), 8)
            ahead = pl.ds(pl.multiple_of(8 * b + 24, 8), 8)
            for f in range(3):
                res[k, f, pl.ds(pl.multiple_of(first + 8 * b, 8), 8), :] = (
                    part[f, rd, 0:128] - from_next(face[f, rd, 0:128], face[f, ahead, 0:128]))

        @pl.when(q < 8)
        def _():
            result_copy(q).start()

        return carry

    def result_copy(q):
        k = lax.div(q, 4) if not isinstance(q, int) else q // 4
        first = pl.multiple_of(PART_ROWS * (lax.rem(q, 4) if not isinstance(q, int) else q % 4), 8)
        rows = pl.ds(first, PART_ROWS)
        return pltpu.make_async_remote_copy(
            src_ref=res.at[k, :, rows, :], dst_ref=res.at[4 + k, :, rows, :], send_sem=send_sem.at[16 + q],
            recv_sem=recv_sem.at[16 + q], device_id=at(3, 0), device_id_type=MESH)

    lax.fori_loop(0, 16, task, 0)
    for q in range(8):
        result_copy(q).wait_recv()

    own_rank = far_rank = jnp.int32(0)
    for s in range(3):
        ident = slots[s]
        mine, _ = owned(ident)
        far = (ident >= 0) & jnp.logical_not(mine)
        index = jnp.where(mine, 2 + own_rank, jnp.where(far, 4 + far_rank, 2))
        index = jnp.minimum(index, 5)
        own_rank = own_rank + jnp.where(mine, 1, 0)
        far_rank = far_rank + jnp.where(far, 1, 0)

        @pl.loop(0, 16, unroll=8)
        def _(b):
            rs = pl.ds(pl.multiple_of(8 * b, 8), 8)
            for f in range(3):
                out[0, 0, s, f, rs, :] = jnp.where(ident >= 0, res[index, f, rs, :], 0.0)

    for copy in copies:
        copy.wait_send()
    for q in range(8):
        result_copy(q).wait_send()


def shards(depth, velocity, bed, slots):
    n = lax.axis_size("rows")
    listed = slots[0, 0]
    vmem = pl.BlockSpec(memory_space=pltpu.VMEM)
    f32 = jnp.float32
    return pl.pallas_call(
        functools.partial(kernel, n),
        out_shape=jax.ShapeDtypeStruct((1, 1, 3, 3, TILE, TILE), f32),
        in_specs=[pl.BlockSpec(memory_space=pltpu.HBM)] * 3 + [pl.BlockSpec(memory_space=pltpu.SMEM)],
        out_specs=vmem,
        scratch_shapes=[
            pltpu.VMEM((256, 256), f32),
            pltpu.VMEM((2, 256, 256), f32),
            pltpu.VMEM((256, 256), f32),
            pltpu.SemaphoreType.DMA((3,)),
            pltpu.VMEM((1, 128), jnp.int32),
            pltpu.VMEM((2, 4, 8, 256), f32),
            pltpu.VMEM((256, 128), f32),
            pltpu.VMEM((2, 4, 8, 128), f32),
            pltpu.VMEM((2, 4, 8, 256), f32),
            pltpu.VMEM((256, 128), f32),
            pltpu.VMEM((2, 4, 8, 128), f32),
            pltpu.VMEM((12, 1, 128), jnp.int32),
            pltpu.SMEM((12, 1, 128), jnp.int32),
            pltpu.VMEM((4, 3, 272, 128), f32),
            pltpu.VMEM((4, 5, 8 * BANDS, 256), f32),
            pltpu.VMEM((5, ROWS + 16, 256), f32),
            pltpu.VMEM((3, ROWS + 16, 256), f32),
            pltpu.VMEM((3, ROWS + 16, 256), f32),
            pltpu.VMEM((3, ROWS + 16, 256), f32),
            pltpu.VMEM((6, 3, TILE, TILE), f32),
            pltpu.SemaphoreType.DMA((24,)),
            pltpu.SemaphoreType.DMA((24,)),
            pltpu.SemaphoreType.DMA,
        ],
        compiler_params=pltpu.CompilerParams(
            collective_id=0, has_side_effects=True, vmem_limit_bytes=VMEM_LIMIT),
    )(depth, velocity, bed, listed)


def solution(mesh):
    in_specs = (
        P(("groups", "rows"), "cols"),
        P(None, ("groups", "rows"), "cols"),
        P(("groups", "rows"), "cols"),
        P(("groups", "rows"), "cols", None),
    )
    out_specs = P(("groups", "rows"), "cols", None, None, None, None)
    return jax.shard_map(shards, mesh=mesh, in_specs=in_specs, out_specs=out_specs, check_vma=False)
```

```python
import functools

import jax
import jax.numpy as jnp
from jax import lax
from jax.experimental import pallas as pl
from jax.experimental.pallas import tpu as pltpu
from jax.sharding import PartitionSpec as P

TILE = 128
RT = 2
CT = 2

GRAVITY = 9.81
TIME_STEP = 0.04
DRY_DEPTH = 0.05
SPEED_FLOOR = 0.5
BANDS = 18
PART_ROWS = 32
PART_BANDS = 6
ROWS = 8 * PART_BANDS
VMEM_LIMIT = 63 * 2**20
MESH = pl.DeviceIdType.MESH


def minmod(a, b):
    return jnp.maximum(jnp.minimum(a, b), 0.0) + jnp.minimum(jnp.maximum(a, b), 0.0)


def face_sweep(own, below, slope, slope_below):
    half = [0.5 * s for s in slope]
    low = [v - s for v, s in zip(own, half)]
    high = [v + 0.5 * s for v, s in zip(below, slope_below)]

    def speeds(h, n, t):
        square = h * h
        w = 2.0 * h / (square + jnp.maximum(square, DRY_DEPTH * DRY_DEPTH))
        return w * n, w * t

    hl, nl, tl, zl = high
    hr, nr, tr, zr = low
    ul, vl = speeds(hl, nl, tl)
    ur, vr = speeds(hr, nr, tr)
    top = jnp.maximum(zl, zr)
    el = jnp.maximum(0.0, hl + zl - top)
    er = jnp.maximum(0.0, hr + zr - top)
    cl = jnp.sqrt(GRAVITY * el)
    cr = jnp.sqrt(GRAVITY * er)
    am = jnp.minimum(jnp.minimum(ul - cl, ur - cr), 0.0)
    ap = jnp.maximum(jnp.maximum(ul + cl, ur + cr), 0.0)
    inv = 1.0 / jnp.maximum(ap - am, SPEED_FLOOR)
    bp = ap * inv
    bm = am * inv
    bb = bp * am
    ml = el * ul
    mr = er * ur
    gl = 0.5 * GRAVITY * el * el
    gr = 0.5 * GRAVITY * er * er
    mass = bp * ml - bm * mr + bb * (er - el)
    push = bp * (ml * ul + gl) - bm * (mr * ur + gr) + bb * (mr - ml)
    side = bp * (ml * vl) - bm * (mr * vr) + bb * (er * vr - el * vl)
    cell_high = own[0] + half[0]
    total = hr + cell_high
    bedterm = 0.5 * GRAVITY * (total * (hr - cell_high) - 2.0 * total * half[3])
    return (mass, push + (bedterm - gr), side), (mass, push - gl, side)


def kernel(n, depth_hbm, vel_hbm, bed_hbm, slots, out,
           depth, vel, bed, in_sem, lists,
           strips, colpack, corner, rowgot, colgot, cornergot, listgot, ids,
           ext, tiles, work, mid, part, face, res,
           send_sem, recv_sem, id_sem):
    g = lax.axis_index("groups")
    r = lax.axis_index("rows")
    c = lax.axis_index("cols")
    peer = 1 - c
    half = n // 2
    shifts = (0, 1, n - 1, half, half + 1, half - 1)
    opposite = (0, 2, 1, 3, 5, 4)
    tile_cols_all = CT * 2

    def at(k, other):
        return (g, lax.rem(r + shifts[k], n), peer if other else c)

    loads = [pltpu.make_async_copy(src, dst, in_sem.at[i]) for i, (src, dst) in enumerate(
        ((depth_hbm, depth), (vel_hbm, vel), (bed_hbm, bed)))]
    for load in loads:
        load.start()
    place = lax.broadcasted_iota(jnp.int32, (1, 128), 1)
    lists[...] = jnp.where(place == 0, slots[0], jnp.where(
        place == 1, slots[1], jnp.where(place == 2, slots[2], -1)))
    barrier = pltpu.get_barrier_semaphore()
    for k in range(6):
        for o in range(2):
            if k or o:
                pl.semaphore_signal(barrier, inc=1, device_id=at(k, o), device_id_type=MESH)

    for load in loads:
        load.wait()
    lane8 = lax.broadcasted_iota(jnp.int32, (8, 128), 1)
    fields = (lambda rs, ls: depth[rs, ls], lambda rs, ls: vel[0, rs, ls],
              lambda rs, ls: vel[1, rs, ls], lambda rs, ls: bed[rs, ls])
    left, right, both = pl.ds(0, 128), pl.ds(128, 128), pl.ds(0, 256)
    for f in range(4):
        for e, rs in enumerate((pl.ds(0, 8), pl.ds(248, 8))):
            strips[e, f] = fields[f](rs, both)
            corner[e, f] = jnp.where(c == 0, fields[f](rs, right), fields[f](rs, left))

    @pl.loop(0, 32, unroll=8)
    def _(b):
        rs = pl.ds(pl.multiple_of(8 * b, 8), 8)
        packed = jnp.zeros((8, 128), jnp.float32)
        for f in range(4):
            slab = jnp.where(c == 0, fields[f](rs, right), fields[f](rs, left))
            packed = jnp.where(lane8 // 8 == f, pltpu.roll(slab, 4 + 8 * f, 1), packed)
        colpack[rs, :] = packed

    pl.semaphore_wait(barrier, 11)

    copies = []

    def send(src, dst, k, o):
        i = len(copies)
        copy = pltpu.make_async_remote_copy(
            src_ref=src, dst_ref=dst, send_sem=send_sem.at[i], recv_sem=recv_sem.at[i],
            device_id=at(k, o), device_id_type=MESH)
        copy.start()
        copies.append(copy)

    send(strips.at[1], rowgot.at[0], 1, 0)
    send(strips.at[0], rowgot.at[1], 2, 0)
    send(corner.at[1], cornergot.at[0], 1, 1)
    send(corner.at[0], cornergot.at[1], 2, 1)
    for k in (3, 0, 1, 2, 4, 5):
        for o in range(2):
            if k or o:
                send(lists, listgot.at[2 * opposite[k] + o], k, o)
    send(colpack, colgot, 0, 1)
    listgot[0] = lists[...]

    @pl.loop(0, 32, unroll=8)
    def _(b):
        rs = pl.ds(pl.multiple_of(8 * b, 8), 8)
        rd = pl.ds(pl.multiple_of(8 * b + 8, 8), 8)
        for j, ls in enumerate((left, right)):
            d = depth[rs, ls]
            ext[0, j, rd, :] = d
            ext[1, j, rd, :] = d * vel[0, rs, ls]
            ext[2, j, rd, :] = d * vel[1, rs, ls]
            ext[3, j, rd, :] = bed[rs, ls]

    for f in range(5):
        work[f, 0:8] = jnp.zeros((8, 256), jnp.float32)
        work[f, ROWS + 8:ROWS + 16] = jnp.zeros((8, 256), jnp.float32)
        if f < 3:
            mid[f, 0:8] = jnp.zeros((8, 256), jnp.float32)
            mid[f, ROWS + 8:ROWS + 16] = jnp.zeros((8, 256), jnp.float32)
            face[f, ROWS + 8:ROWS + 16] = jnp.zeros((8, 256), jnp.float32)

    for copy in copies:
        copy.wait_recv()
    to_ids = pltpu.make_async_copy(listgot, ids, id_sem)
    to_ids.start()

    def put(j, rd, d, a, b, z, keep):
        d = jnp.where(keep, d, 0.0)
        ext[0, j, rd, :] = d
        ext[1, j, rd, :] = d * a
        ext[2, j, rd, :] = d * b
        ext[3, j, rd, :] = jnp.where(keep, z, 0.0)

    for e, (rd, keep) in enumerate(((pl.ds(0, 8), r > 0), (pl.ds(264, 8), r < n - 1))):
        for j, ls in enumerate((left, right)):
            put(j, rd, *(rowgot[e, f, :, ls] for f in range(4)), keep)
        put(2, rd, *(cornergot[e, f] for f in range(4)), keep)

    @pl.loop(0, 32, unroll=8)
    def _(b):
        rs = pl.ds(pl.multiple_of(8 * b, 8), 8)
        rd = pl.ds(pl.multiple_of(8 * b + 8, 8), 8)
        got = colgot[rs, :]
        put(2, rd, *(pltpu.roll(got, 128 - (4 + 8 * f), 1) for f in range(4)), True)

    to_ids.wait()

    def is_active(a, b):
        row = RT * r - 1 + a
        col = CT * c - 1 + b
        inside = (row >= 0) & (row < RT * n) & (col >= 0) & (col < tile_cols_all)
        ident = row * tile_cols_all + col
        k = {0: 2, 1: 0, 2: 0, 3: 1}[a]
        o = 0 if b in (1, 2) else 1
        partner = {0: 3, 1: 4, 2: 5}[k]
        hit = ids[2 * k + o, 0, 0] == ident
        for q in (k, partner):
            for s in range(3):
                hit = hit | (ids[2 * q + o, 0, s] == ident)
        return jnp.where(hit & inside, 1.0, 0.0)

    active = [[is_active(a, b) for b in range(4)] for a in range(4)]
    lower = lane8 < 64
    at_left = (c == 0)
    for i in range(2):
        for j in range(2):
            t = 2 * i + j

            def row_of(a):
                return jnp.broadcast_to(active[a][j + 1], (8, 128)), jnp.where(
                    lower, active[a][j + 2], active[a][j])

            top, middle, bottom = row_of(i), row_of(i + 1), row_of(i + 2)

            @pl.loop(0, BANDS, unroll=6)
            def _(b):
                rs = pl.ds(pl.multiple_of(8 * b, 8), 8)
                rd = pl.ds(pl.multiple_of(8 * b + 128 * i, 8), 8)
                for f in range(4):
                    tiles[t, f, rs, 0:128] = ext[f, j, rd, :]
                    outer = ext[f, 2, rd, :]
                    inner = ext[f, 1 - j, rd, :]
                    if j == 0:
                        tiles[t, f, rs, 128:256] = jnp.where(
                            lower, inner, jnp.where(at_left, 0.0, outer))
                    else:
                        tiles[t, f, rs, 128:256] = jnp.where(
                            lower, jnp.where(at_left, outer, 0.0), inner)
                for h in range(2):
                    tiles[t, 4, rs, 128 * h:128 * h + 128] = jnp.where(
                        b == 0, top[h], jnp.where(b == BANDS - 1, bottom[h], middle[h]))

    def owned(ident):
        safe = jnp.maximum(ident, 0)
        row = lax.div(safe, tile_cols_all)
        col = lax.rem(safe, tile_cols_all)
        mine = (ident >= 0) & (lax.div(row, RT) == r) & (lax.div(col, CT) == c)
        return mine, lax.rem(row, RT) * CT + lax.rem(col, CT)

    def ranked(entries):
        first = second = count = jnp.int32(0)
        for ident in entries:
            mine, tile = owned(ident)
            first = jnp.where(mine & (count == 0), tile, first)
            second = jnp.where(mine & (count == 1), tile, second)
            count = count + jnp.where(mine, 1, 0)
        return first, second

    sent = ranked([ids[6, 0, s] for s in range(3)])
    kept = ranked([slots[s] for s in range(3)])

    row8 = lax.broadcasted_iota(jnp.int32, (8, 256), 0)

    def from_next(cur, nxt):
        edge = row8[:, :cur.shape[1]] == 7
        return jnp.where(edge, pltpu.roll(nxt, 7, 0), pltpu.roll(cur, 7, 0))

    def step(src, bed_ref):
        refs = [src.at[0], src.at[1], src.at[2], bed_ref]
        order = (0, 2, 1, 3)

        def band(b, carry):
            prev_down, prev_slope = carry
            base = pl.multiple_of(8 * b + 8, 8)
            here = pl.ds(base, 8)
            ahead = pl.ds(pl.multiple_of(8 * b + 16, 8), 8)
            v0 = [ref[here, :] for ref in refs]
            down = [pltpu.roll(v, 1, 0) for v in v0]
            vm = [jnp.where(row8 == 0, p, d) for p, d in zip(prev_down, down)]
            vp = [from_next(v, ref[ahead, :]) for v, ref in zip(v0, refs)]
            slope = [minmod(v - m, p - v) for v, m, p in zip(v0, vm, vp)]
            turned = [pltpu.roll(q, 1, 0) for q in slope]
            slope_below = [jnp.where(row8 == 0, p, d) for p, d in zip(prev_slope, turned)]
            pick = lambda vs: [vs[q] for q in order]
            gain, loss = face_sweep(pick(v0), pick(vm), pick(slope), pick(slope_below))
            for q in range(3):
                face[q, here, :] = TIME_STEP * loss[order[q]]
            left_of = [pltpu.roll(v, 1, 1) for v in v0]
            diff = [x - y for x, y in zip(v0, left_of)]
            across = [minmod(d, pltpu.roll(d, 255, 1)) for d in diff]
            across_left = [pltpu.roll(q, 1, 1) for q in across]
            xgain, xloss = face_sweep(v0, left_of, across, across_left)
            for q in range(3):
                part[q, here, :] = v0[q] + TIME_STEP * (
                    xgain[q] + gain[order[q]] - pltpu.roll(xloss[q], 255, 1))
            return down, turned

        zeros = [jnp.zeros((8, 256), jnp.float32)] * 4
        lax.fori_loop(0, PART_BANDS, band, (zeros, zeros), unroll=6)

    def task(q, carry):
        k = lax.div(q, 4)
        first = PART_ROWS * lax.rem(q, 4)
        t = jnp.where(k == 0, sent[0], jnp.where(k == 1, sent[1], jnp.where(k == 2, kept[0], kept[1])))

        @pl.loop(0, PART_BANDS, unroll=6)
        def _(b):
            rs = pl.ds(pl.multiple_of(first + 8 * b, 8), 8)
            rd = pl.ds(pl.multiple_of(8 * b + 8, 8), 8)
            for f in range(5):
                work[f, rd, :] = tiles[t, f, rs, :]

        step(work, work.at[3])

        @pl.loop(0, PART_BANDS, unroll=6)
        def _(b):
            rd = pl.ds(pl.multiple_of(8 * b + 8, 8), 8)
            ahead = pl.ds(pl.multiple_of(8 * b + 16, 8), 8)
            keep = work[4, rd, :] > 0.5
            for f in range(3):
                mid[f, rd, :] = jnp.where(
                    keep, part[f, rd, :] - from_next(face[f, rd, :], face[f, ahead, :]), work[f, rd, :])

        step(mid, work.at[3])

        @pl.loop(0, 4, unroll=4)
        def _(b):
            rd = pl.ds(pl.multiple_of(8 * b + 16, 8), 8)
            ahead = pl.ds(pl.multiple_of(8 * b + 24, 8), 8)
            for f in range(3):
                res[k, f, pl.ds(pl.multiple_of(first + 8 * b, 8), 8), :] = (
                    part[f, rd, 0:128] - from_next(face[f, rd, 0:128], face[f, ahead, 0:128]))

        @pl.when(q < 8)
        def _():
            result_copy(q).start()

        return carry

    def result_copy(q):
        k = lax.div(q, 4) if not isinstance(q, int) else q // 4
        first = pl.multiple_of(PART_ROWS * (lax.rem(q, 4) if not isinstance(q, int) else q % 4), 8)
        rows = pl.ds(first, PART_ROWS)
        return pltpu.make_async_remote_copy(
            src_ref=res.at[k, :, rows, :], dst_ref=res.at[4 + k, :, rows, :], send_sem=send_sem.at[16 + q],
            recv_sem=recv_sem.at[16 + q], device_id=at(3, 0), device_id_type=MESH)

    lax.fori_loop(0, 16, task, 0)
    for q in range(8):
        result_copy(q).wait_recv()

    own_rank = far_rank = jnp.int32(0)
    for s in range(3):
        ident = slots[s]
        mine, _ = owned(ident)
        far = (ident >= 0) & jnp.logical_not(mine)
        index = jnp.where(mine, 2 + own_rank, jnp.where(far, 4 + far_rank, 2))
        index = jnp.minimum(index, 5)
        own_rank = own_rank + jnp.where(mine, 1, 0)
        far_rank = far_rank + jnp.where(far, 1, 0)

        @pl.loop(0, 16, unroll=8)
        def _(b):
            rs = pl.ds(pl.multiple_of(8 * b, 8), 8)
            for f in range(3):
                out[0, 0, s, f, rs, :] = jnp.where(ident >= 0, res[index, f, rs, :], 0.0)

    for copy in copies:
        copy.wait_send()
    for q in range(8):
        result_copy(q).wait_send()


def shards(depth, velocity, bed, slots):
    n = lax.axis_size("rows")
    listed = slots[0, 0]
    vmem = pl.BlockSpec(memory_space=pltpu.VMEM)
    f32 = jnp.float32
    return pl.pallas_call(
        functools.partial(kernel, n),
        out_shape=jax.ShapeDtypeStruct((1, 1, 3, 3, TILE, TILE), f32),
        in_specs=[pl.BlockSpec(memory_space=pltpu.HBM)] * 3 + [pl.BlockSpec(memory_space=pltpu.SMEM)],
        out_specs=vmem,
        scratch_shapes=[
            pltpu.VMEM((256, 256), f32),
            pltpu.VMEM((2, 256, 256), f32),
            pltpu.VMEM((256, 256), f32),
            pltpu.SemaphoreType.DMA((3,)),
            pltpu.VMEM((1, 128), jnp.int32),
            pltpu.VMEM((2, 4, 8, 256), f32),
            pltpu.VMEM((256, 128), f32),
            pltpu.VMEM((2, 4, 8, 128), f32),
            pltpu.VMEM((2, 4, 8, 256), f32),
            pltpu.VMEM((256, 128), f32),
            pltpu.VMEM((2, 4, 8, 128), f32),
            pltpu.VMEM((12, 1, 128), jnp.int32),
            pltpu.SMEM((12, 1, 128), jnp.int32),
            pltpu.VMEM((4, 3, 272, 128), f32),
            pltpu.VMEM((4, 5, 8 * BANDS, 256), f32),
            pltpu.VMEM((5, ROWS + 16, 256), f32),
            pltpu.VMEM((3, ROWS + 16, 256), f32),
            pltpu.VMEM((3, ROWS + 16, 256), f32),
            pltpu.VMEM((3, ROWS + 16, 256), f32),
            pltpu.VMEM((6, 3, TILE, TILE), f32),
            pltpu.SemaphoreType.DMA((24,)),
            pltpu.SemaphoreType.DMA((24,)),
            pltpu.SemaphoreType.DMA,
        ],
        compiler_params=pltpu.CompilerParams(
            collective_id=0, has_side_effects=True, vmem_limit_bytes=VMEM_LIMIT),
    )(depth, velocity, bed, listed)


def solution(mesh):
    in_specs = (
        P(("groups", "rows"), "cols"),
        P(None, ("groups", "rows"), "cols"),
        P(("groups", "rows"), "cols"),
        P(("groups", "rows"), "cols", None),
    )
    out_specs = P(("groups", "rows"), "cols", None, None, None, None)
    return jax.shard_map(shards, mesh=mesh, in_specs=in_specs, out_specs=out_specs, check_vma=False)
```
